32 devices in a mesh: groups: 2 (over y), expert: 8 (over z, core), sub: 2 (over x).
Axes of the slice: x: 2, y: 2, z: 4, core: 2. Of those that a mesh axis runs over, the one named last changes fastest.
Arguments:
- latent: bfloat16 [4096, 1024], P(('groups', 'expert', 'sub')), parts along dimension 0, may hold values from -6 to 6
- routes: int32 [4096, 4], P(('groups', 'expert', 'sub')), parts along dimension 0, may hold values from 0 to 7, all different within a row; in each aligned block of 128 rows (0 to 127, 128 to 255, ...) at most 96 rows name the same one
- gates: float32 [4096, 4], P(('groups', 'expert', 'sub')), parts along dimension 0, may hold values from 0.1 to 1
- up_weight: bfloat16 [8, 1024, 2688], P('expert', None, 'sub'), may hold values from -0.1875 to 0.1875
- down_weight: bfloat16 [8, 1024, 2688], P('expert', None, 'sub'), may hold values from -0.125 to 0.125
Outputs:
- mixed: bfloat16 [4096, 1024], P(('groups', 'expert', 'sub')), parts along dimension 0
The draws below stay inside these ranges and needn't reach their ends.
There are 2 independent parts, one for each index of `groups`. The reference program is written for one: setup_inputs(seed, part) draws one part's arguments, and reference() takes and returns one part's arrays. A program takes and returns all parts, laid end to end along the dimension named above; an argument that names none is the same for every part. Nothing has to cross between parts.
Inputs may be any that keep to these rules, and one draw needn't show every extreme that they name: `routes`: each token names 4 different experts; among the 128 tokens of one device no expert is named more than 96 times, a bound that some block reaches.
All inputs are finite; a program needn't handle non-finite values.
Results may differ from the reference program's by a relative error of at most 0.0058.
Values may be sent and summed in bfloat16 or wider, within the bound.
No kernel may reach another device: no remote copies, remote signals or barrier semaphores. Data moves between devices by JAX's collectives and lax.ppermute only.
A program may use at most 128 MiB of HBM per device.

```python
import math
import jax
import jax.numpy as jnp
import numpy as np
from jax import lax

LATENT = 1024
HIDDEN_SIZE = 2688
TOK_DEV = 128
TOPK = 4
EXPERTS = 8
MOST = 96
TOKENS = 2048


def levels(key, shape, split, least, high):
    loudness = 1.0
    for axis_at, parts in split:
        steps = jax.random.uniform(jax.random.fold_in(jax.random.fold_in(key, 6), axis_at), (parts,), jnp.float32, least / len(split), high / len(split))
        loudness = loudness * jnp.repeat(jnp.exp(steps), shape[axis_at] // parts).reshape((-1,) + (1,) * (len(shape) - 1 - axis_at))
    return loudness


def shared_out(stream_key, own, number, rows, number_of, top, limit, slope):
    order = jax.random.permutation(stream_key, number_of)
    heavy_load, ordinary = load_shares(number_of, rows * top, limit, slope, True), load_shares(number_of, rows * top, limit, slope, False)
    places = jnp.arange(number_of)

    def named(tallies, offset_by):
        used = int((tallies > 0).sum())
        fixed = max(1, used // 4)
        shifted = fixed + (places - fixed + offset_by * (used - fixed)) % max(1, number_of - fixed)
        return jnp.zeros((number_of,), jnp.int32).at[order[jnp.where(places < fixed, places, shifted)]].set(jnp.asarray(tallies, jnp.int32))

    tallies = jnp.where(number % 4 == 0, named(heavy_load, number // 4), named(ordinary, number - number // 4 - 1))
    mixed = jax.random.permutation(jax.random.fold_in(own, 3), number_of)
    donor, receiver = mixed[0:number_of // 2 * 2:2], mixed[1:number_of // 2 * 2:2]
    margin = jnp.minimum(tallies[donor] - 1, limit - tallies[receiver]) // 2
    margin = jnp.where((donor == order[0]) | (receiver == order[0]) | (tallies[receiver] == 0), 0, jnp.maximum(margin, 0))
    shifted = jax.random.randint(jax.random.fold_in(own, 4), (number_of // 2,), 0, 1 << 20) % (margin + 1)
    tallies = tallies.at[donor].add(-shifted).at[receiver].add(shifted)
    members = jnp.searchsorted(jnp.cumsum(tallies), jnp.arange(rows * top), side="right").astype(jnp.int32)
    listing = members.reshape(top, rows).T
    listing = listing[jax.random.permutation(jax.random.fold_in(own, 1), rows)]
    offset_by = jax.random.randint(jax.random.fold_in(own, 2), (rows, 1), 0, top)
    return jnp.take_along_axis(listing, (jnp.arange(top)[None, :] + offset_by) % top, axis=1)


def load_shares(amount, total, limit, lean, full):
    weights = [(1 << 20) // math.isqrt(grade ** lean) + 1 for grade in range(1, amount + 1)]
    largest = limit if full else min(limit, max(-(-total // amount), total * weights[0] // sum(weights)))
    least = 1 if total - largest >= amount - 1 else 0
    given, rest = [largest] + [least] * (amount - 1), total - largest - least * (amount - 1)
    while rest > 0:
        movable = [i for i in range(1, amount) if given[i] < largest] or [i for i in range(1, amount) if given[i] < limit]
        pool, left = sum([weights[i] for i in movable]), rest
        for i in movable:
            more = min(limit - given[i], max(1, left * weights[i] // pool), rest)
            given[i] = given[i] + more
            rest = rest - more
    return np.array(given)


def centred(key, extent, spread, reach, split=(), kind=jnp.bfloat16):
    array = spread * jax.random.normal(key, extent, jnp.float32)
    if split:
        array = array * levels(key, extent, split, -0.22, 0.18)
    return jnp.clip(array, -reach, reach).astype(kind)


def setup_inputs(seed: int = 0, part: int = 0) -> dict:
    key_of = jax.random.split(jax.random.key(seed), 6)
    part_keys = jax.random.split(jax.random.fold_in(key_of[5], part), 6)
    latent = centred(part_keys[0], (TOKENS, LATENT), 1.0, 6.0, ((0, 16),))
    routes_keys = jax.random.split(jax.random.fold_in(part_keys[1], 1), TOKENS // TOK_DEV)
    routes_turns = jax.random.permutation(jax.random.fold_in(part_keys[1], 3), TOKENS // TOK_DEV)
    routes = jax.vmap(lambda own, number: shared_out(jax.random.fold_in(part_keys[1], 2), own, number, TOK_DEV, EXPERTS, TOPK, MOST, 2))(routes_keys, routes_turns).reshape((TOKENS, TOPK))
    gates = jnp.clip(0.1 + 0.9 * jax.random.uniform(part_keys[2], (TOKENS, TOPK), jnp.float32) ** levels(part_keys[2], (TOKENS, TOPK), ((0, 16),), -0.2, 0.2), 0.1, 1.0)
    up_weight = centred(key_of[3], (EXPERTS, LATENT, HIDDEN_SIZE), LATENT ** -0.5, 0.1875, ((0, 8), (2, 2)))
    down_weight = centred(key_of[4], (EXPERTS, LATENT, HIDDEN_SIZE), HIDDEN_SIZE ** -0.5, 0.125, ((0, 8), (2, 2)))
    return dict(latent=latent, routes=routes, gates=gates, up_weight=up_weight, down_weight=down_weight)


def expert_rows(gathered, up_part, down_part):
    preact = jnp.dot(gathered, up_part, preferred_element_type=jnp.float32)
    active = jnp.square(jnp.maximum(preact, 0.0)).astype(jnp.bfloat16)
    return lax.dot_general(active, down_part, (((1,), (1,)), ((), ())), preferred_element_type=jnp.float32)


def reference(latent, routes, gates, up_weight, down_weight):
    pair_count = TOKENS * TOPK
    route_ids = routes.reshape(-1).astype(jnp.int32)
    tok_index = jnp.arange(pair_count, dtype=jnp.int32) // TOPK
    flat_gate = gates.reshape(-1)
    padded = jnp.concatenate([latent, jnp.zeros((1, LATENT), latent.dtype)], axis=0)
    capacity = (TOKENS // TOK_DEV) * MOST

    def one_expert(carry, expert):
        chosen = jnp.nonzero(route_ids == expert, size=capacity, fill_value=pair_count)[0].astype(jnp.int32)
        is_live = chosen < pair_count
        clipped = jnp.minimum(chosen, pair_count - 1).astype(jnp.int32)
        token_of = jnp.where(is_live, tok_index[clipped], TOKENS).astype(jnp.int32)
        gathered = padded[token_of]
        rounded = expert_rows(gathered, up_weight[expert], down_weight[expert]).astype(jnp.bfloat16)
        rounded = lax.optimization_barrier(rounded).astype(jnp.float32)
        weight = jnp.where(is_live, flat_gate[clipped], jnp.float32(0.0))
        carry = carry.at[token_of].add(weight[:, None] * rounded)
        return carry, None

    summed = lax.scan(one_expert, jnp.zeros((TOKENS + 1, LATENT), jnp.float32), jnp.arange(EXPERTS, dtype=jnp.int32))[0]
    return summed[:TOKENS].astype(jnp.bfloat16)
```

```python
import functools
import math

import jax
import jax.numpy as jnp
from jax import lax
from jax.experimental import pallas as pl
from jax.experimental.pallas import tpu as pltpu
from jax.sharding import PartitionSpec as P


def expert_kernel(block, slots, unit, w_ref, x_ref, up_ref, down_ref, out_ref):
    blocks = w_ref.shape[1]
    weight = w_ref[0]
    named = (weight > 0).astype(jnp.bfloat16)
    earlier = lax.broadcasted_iota(jnp.int32, (block, block), 0)
    later = lax.broadcasted_iota(jnp.int32, (block, block), 1)
    before = (earlier < later).astype(jnp.bfloat16)
    rank = jnp.dot(named, before, preferred_element_type=jnp.float32).astype(jnp.int32)
    picks, scales, rows = [], [], []
    for u in range(blocks // unit):
        slot = lax.broadcasted_iota(jnp.int32, (unit * slots, block), 0)
        parts = []
        scale = 0.0
        for j in range(unit):
            b = u * unit + j
            here = (slot == rank[b : b + 1] + j * slots) & (weight[b : b + 1] > 0)
            scale = scale + jnp.sum(jnp.where(here, weight[b : b + 1], 0.0), axis=1, keepdims=True)
            parts.append(here.astype(jnp.bfloat16))
        pick = jnp.concatenate(parts, axis=1) if unit > 1 else parts[0]
        tokens = x_ref[u * unit * block : (u + 1) * unit * block, :]
        rows.append(jnp.dot(pick, tokens, preferred_element_type=jnp.float32).astype(jnp.bfloat16))
        picks.append(pick)
        scales.append(scale)
    picked = jnp.concatenate(rows, axis=0)
    preact = jnp.dot(picked, up_ref[0], preferred_element_type=jnp.float32)
    active = jnp.square(jnp.maximum(preact, 0.0)).astype(jnp.bfloat16)
    summed = lax.dot_general(
        active, down_ref[0], (((1,), (1,)), ((), ())), preferred_element_type=jnp.float32
    )
    size = unit * slots
    for u in range(blocks // unit):
        gated = (summed[u * size : (u + 1) * size] * scales[u]).astype(jnp.bfloat16)
        out_ref[u * unit * block : (u + 1) * unit * block, :] = lax.dot_general(
            picks[u], gated, (((0,), (0,)), ((), ())), preferred_element_type=jnp.float32
        ).astype(jnp.bfloat16)


def run_expert(weight, rows, up_weight, down_weight, block, slots):
    total, width = rows.shape
    hidden = up_weight.shape[2]
    unit = 16 // math.gcd(16, slots)
    blocks = total // block
    each = unit
    while each * 2 <= blocks and blocks % (each * 2) == 0 and each * 2 * slots <= 512:
        each *= 2
    steps = blocks // each
    return pl.pallas_call(
        functools.partial(expert_kernel, block, slots, unit),
        grid=(steps,),
        out_shape=jax.ShapeDtypeStruct((total, width), jnp.bfloat16),
        in_specs=[
            pl.BlockSpec((1, each, block), lambda i: (i, 0, 0)),
            pl.BlockSpec((each * block, width), lambda i: (i, 0)),
            pl.BlockSpec((1, width, hidden), lambda i: (0, 0, 0)),
            pl.BlockSpec((1, width, hidden), lambda i: (0, 0, 0)),
        ],
        out_specs=pl.BlockSpec((each * block, width), lambda i: (i, 0)),
        compiler_params=pltpu.CompilerParams(vmem_limit_bytes=48 * 1024 * 1024),
        cost_estimate=pl.CostEstimate(
            flops=4 * blocks * slots * width * (hidden + block),
            bytes_accessed=4 * total * width + 4 * width * hidden,
            transcendentals=0,
        ),
    )(weight.reshape(steps, each, block), rows, up_weight, down_weight)


def local(latent, routes, gates, up_weight, down_weight):
    block, width = latent.shape
    top = routes.shape[1]
    experts = lax.axis_size("expert")
    slots = min(block, 3 * block * top // (2 * experts))
    rows = lax.all_gather(latent, ("expert", "sub"), axis=0, tiled=True)
    ids = jnp.arange(experts, dtype=jnp.int32)
    weight = jnp.sum(
        jnp.where(routes.T[None] == ids[:, None, None], gates.T[None], 0.0), axis=1
    )
    weights = lax.all_gather(weight, ("expert", "sub"), axis=0, tiled=False)
    mine = lax.dynamic_index_in_dim(weights, lax.axis_index("expert"), 1, keepdims=False)
    partial = run_expert(mine, rows, up_weight, down_weight, block, slots)
    return lax.psum_scatter(partial, ("expert", "sub"), scatter_dimension=0, tiled=True)


def solution(mesh):
    placed = (
        P(("groups", "expert", "sub"), None),
        P(("groups", "expert", "sub"), None),
        P(("groups", "expert", "sub"), None),
        P("expert", None, "sub"),
        P("expert", None, "sub"),
    )
    return jax.shard_map(
        local,
        mesh=mesh,
        in_specs=placed,
        out_specs=P(("groups", "expert", "sub"), None),
        check_vma=False,
    )
```

```python
import functools
import math

import jax
import jax.numpy as jnp
from jax import lax
from jax.experimental import pallas as pl
from jax.experimental.pallas import tpu as pltpu
from jax.sharding import Mesh, PartitionSpec as P

CORES = 2
NT = (((1,), (1,)), ((), ()))
TN = (((0,), (0,)), ((), ()))


def expert_kernel(block, slots, unit, w_ref, x_ref, *refs):
    out_ref = refs[-1]
    blocks = w_ref.shape[2]
    earlier = lax.broadcasted_iota(jnp.int32, (block, block), 0)
    later = lax.broadcasted_iota(jnp.int32, (block, block), 1)
    before = (earlier < later).astype(jnp.bfloat16)
    size = unit * slots
    slot = lax.broadcasted_iota(jnp.int32, (size, block), 0)
    sums = [0.0] * (blocks // unit)
    for n in range(w_ref.shape[0]):
        up_ref, down_ref = refs[2 * n], refs[2 * n + 1]
        weight = w_ref[n, 0]
        named = (weight > 0).astype(jnp.bfloat16)
        rank = jnp.dot(named, before, preferred_element_type=jnp.float32).astype(jnp.int32)
        picks, scales, rows = [], [], []
        for u in range(blocks // unit):
            parts = []
            scale = 0.0
            for j in range(unit):
                b = u * unit + j
                here = (slot == rank[b : b + 1] + j * slots) & (weight[b : b + 1] > 0)
                scale = scale + jnp.sum(
                    jnp.where(here, weight[b : b + 1], 0.0), axis=1, keepdims=True
                )
                parts.append(here.astype(jnp.bfloat16))
            pick = jnp.concatenate(parts, axis=1) if unit > 1 else parts[0]
            tokens = x_ref[u * unit * block : (u + 1) * unit * block, :]
            rows.append(
                jnp.dot(pick, tokens, preferred_element_type=jnp.float32).astype(jnp.bfloat16)
            )
            picks.append(pick)
            scales.append(scale)
        picked = jnp.concatenate(rows, axis=0)
        preact = lax.dot_general(picked, up_ref[0], NT, preferred_element_type=jnp.float32)
        active = jnp.square(jnp.maximum(preact, 0.0)).astype(jnp.bfloat16)
        summed = jnp.dot(active, down_ref[0], preferred_element_type=jnp.float32)
        for u in range(blocks // unit):
            gated = (summed[u * size : (u + 1) * size] * scales[u]).astype(jnp.bfloat16)
            sums[u] = sums[u] + lax.dot_general(
                picks[u], gated, TN, preferred_element_type=jnp.float32
            )
    for u in range(blocks // unit):
        out_ref[u * unit * block : (u + 1) * unit * block, :] = sums[u].astype(jnp.bfloat16)


def run_experts(weights, rows, tables, block, slots):
    total, width = rows.shape
    number = weights.shape[0]
    hidden = tables[0].shape[1]
    unit = 16 // math.gcd(16, slots)
    blocks = total // block
    each = unit
    while blocks % (each * 2) == 0 and each * 2 * slots <= 512:
        each *= 2
    steps = blocks // each
    return pl.pallas_call(
        functools.partial(expert_kernel, block, slots, unit),
        grid=(steps,),
        out_shape=jax.ShapeDtypeStruct((total, width), jnp.bfloat16),
        in_specs=[
            pl.BlockSpec((number, 1, each, block), lambda i: (0, i, 0, 0)),
            pl.BlockSpec((each * block, width), lambda i: (i, 0)),
        ]
        + [pl.BlockSpec(memory_space=pltpu.VMEM)] * len(tables),
        out_specs=pl.BlockSpec((each * block, width), lambda i: (i, 0)),
        compiler_params=pltpu.CompilerParams(vmem_limit_bytes=56 * 1024 * 1024),
        cost_estimate=pl.CostEstimate(
            flops=4 * number * blocks * slots * width * (hidden + block),
            bytes_accessed=4 * total * width + 2 * len(tables) * width * hidden,
            transcendentals=0,
        ),
    )(weights.reshape(number, steps, each, block), rows, *tables)


def local(latent, routes, gates, up_weight, down_weight):
    block, width = latent.shape
    top = routes.shape[1]
    cores = lax.axis_size("core")
    experts = lax.axis_size("z") * cores
    slots = min(block, 3 * block * top // (2 * experts))
    own_up, own_down = jnp.swapaxes(up_weight, 1, 2), jnp.swapaxes(down_weight, 1, 2)
    rows = lax.all_gather(latent, ("z", "sub"), axis=0, tiled=True)
    tables = [own_up, own_down]
    for step in range(1, cores):
        turn = [(c, (c + step) % cores) for c in range(cores)]
        tables += [lax.ppermute(own_up, "core", turn), lax.ppermute(own_down, "core", turn)]
    ids = jnp.arange(experts, dtype=jnp.int32)
    weight = jnp.sum(
        jnp.where(routes.T[None] == ids[:, None, None], gates.T[None], 0.0), axis=1
    )
    weights = lax.all_gather(weight, ("z", "sub"), axis=1, tiled=False)
    first, core = lax.axis_index("z") * cores, lax.axis_index("core")
    mine = jnp.stack(
        [
            lax.dynamic_index_in_dim(weights, first + (core + cores - s) % cores, 0, keepdims=False)
            for s in range(cores)
        ]
    )
    partial = run_experts(mine, rows, tables, block, slots)
    return lax.psum_scatter(partial, ("z", "sub"), scatter_dimension=0, tiled=True)


def solution(mesh):
    groups, experts, sub = (mesh.shape[a] for a in ("groups", "expert", "sub"))
    inner = Mesh(
        mesh.devices.reshape(groups, experts // CORES, CORES, sub),
        ("groups", "z", "core", "sub"),
    )
    tokens = P(("groups", "z", "core", "sub"), None)
    table = P(("z", "core"), None, "sub")
    return jax.shard_map(
        local,
        mesh=inner,
        in_specs=(tokens, tokens, tokens, table, table),
        out_specs=tokens,
        check_vma=False,
    )
```

```python
import functools
import math

import jax
import jax.numpy as jnp
from jax import lax
from jax.experimental import pallas as pl
from jax.experimental.pallas import tpu as pltpu
from jax.sharding import Mesh, PartitionSpec as P

CORES = 2
ROUNDS = 2
TERMS = 3
NT = (((1,), (1,)), ((), ()))
TN = (((0,), (0,)), ((), ()))


def pack_kernel(experts, extra, latent_ref, routes_ref, gates_ref, out_ref):
    block, width = latent_ref.shape
    out_ref[:block, :] = latent_ref[...]
    ids = lax.broadcasted_iota(jnp.int32, (extra, block), 0)
    weight = jnp.zeros((extra, block), jnp.float32)
    for k in range(routes_ref.shape[0]):
        weight = weight + jnp.where(routes_ref[k : k + 1, :] == ids, gates_ref[k : k + 1, :], 0.0)
    out_ref[block:, :] = jnp.zeros((extra, width), jnp.bfloat16)
    for t in range(TERMS):
        term = weight.astype(jnp.bfloat16)
        out_ref[block:, t * block : (t + 1) * block] = term
        weight = weight - term.astype(jnp.float32)


def pack(latent, routes, gates, experts):
    block, width = latent.shape
    extra = -(-experts // 16) * 16
    return pl.pallas_call(
        functools.partial(pack_kernel, experts, extra),
        out_shape=jax.ShapeDtypeStruct((block + extra, width), jnp.bfloat16),
        in_specs=[pl.BlockSpec(memory_space=pltpu.VMEM)] * 3,
        out_specs=pl.BlockSpec(memory_space=pltpu.VMEM),
    )(latent, routes.T, gates.T)


def expert_kernel(block, slots, unit, number, blocks, ids_ref, after_ref, *refs):
    x_refs, tables, out_refs = refs[:blocks], refs[blocks : blocks + 2 * number], refs[blocks + 2 * number :]
    extra = x_refs[0].shape[0] - block
    earlier = lax.broadcasted_iota(jnp.int32, (block, block), 0)
    later = lax.broadcasted_iota(jnp.int32, (block, block), 1)
    before = (earlier < later).astype(jnp.bfloat16)
    size = unit * slots
    slot = lax.broadcasted_iota(jnp.int32, (size, block), 0)
    row = lax.broadcasted_iota(jnp.int32, (extra, block), 0)
    gates, ranks = [], []
    for x_ref in x_refs:
        gate = 0.0
        for t in range(TERMS):
            gate = gate + x_ref[block:, t * block : (t + 1) * block].astype(jnp.float32)
        gates.append(gate)
        ranks.append(
            jnp.dot((gate > 0).astype(jnp.bfloat16), before, preferred_element_type=jnp.float32)
        )
    sums = [0.0] * blocks
    for n in range(number):
        up_ref, down_ref = tables[2 * n], tables[2 * n + 1]
        mine = row == ids_ref[n]
        picks, scales, rows = [], [], []
        for u in range(blocks // unit):
            parts = []
            scale = 0.0
            for j in range(unit):
                b = u * unit + j
                weight = jnp.sum(jnp.where(mine, gates[b], 0.0), axis=0, keepdims=True)
                rank = jnp.sum(jnp.where(mine, ranks[b], 0.0), axis=0, keepdims=True)
                here = (slot == rank.astype(jnp.int32) + j * slots) & (weight > 0)
                scale = scale + jnp.sum(jnp.where(here, weight, 0.0), axis=1, keepdims=True)
                parts.append(here.astype(jnp.bfloat16))
            tokens = [x_refs[u * unit + j][:block, :] for j in range(unit)]
            pick = jnp.concatenate(parts, axis=1) if unit > 1 else parts[0]
            token = jnp.concatenate(tokens, axis=0) if unit > 1 else tokens[0]
            rows.append(
                jnp.dot(pick, token, preferred_element_type=jnp.float32).astype(jnp.bfloat16)
            )
            picks.append(parts)
            scales.append(scale)
        picked = jnp.concatenate(rows, axis=0)
        preact = lax.dot_general(picked, up_ref[0], NT, preferred_element_type=jnp.float32)
        active = jnp.square(jnp.maximum(preact, 0.0)).astype(jnp.bfloat16)
        summed = jnp.dot(active, down_ref[0], preferred_element_type=jnp.float32)
        for u in range(blocks // unit):
            gated = (summed[u * size : (u + 1) * size] * scales[u]).astype(jnp.bfloat16)
            for j in range(unit):
                b = u * unit + j
                sums[b] = sums[b] + lax.dot_general(
                    picks[u][j], gated, TN, preferred_element_type=jnp.float32
                )
    for b in range(blocks):
        out_refs[b][...] = sums[b].astype(out_refs[b].dtype)


def run_experts(ids, after, arrived, tables, kinds, block, slots):
    blocks, number = len(arrived), len(tables) // 2
    hidden, width = tables[0].shape[1:]
    unit = 16 // math.gcd(16, slots)
    whole = pl.BlockSpec(memory_space=pltpu.VMEM)
    return pl.pallas_call(
        functools.partial(expert_kernel, block, slots, unit, number, blocks),
        out_shape=[jax.ShapeDtypeStruct((block, width), kind) for kind in kinds],
        in_specs=[pl.BlockSpec(memory_space=pltpu.SMEM), pl.BlockSpec(memory_space=pl.ANY)]
        + [whole] * (blocks + len(tables)),
        out_specs=[whole] * blocks,
        compiler_params=pltpu.CompilerParams(vmem_limit_bytes=34 * 1024 * 1024),
        cost_estimate=pl.CostEstimate(
            flops=4 * number * blocks * slots * width * (hidden + block),
            bytes_accessed=5 * blocks * block * width + 2 * len(tables) * width * hidden,
            transcendentals=0,
        ),
    )(ids, after, *arrived, *tables)


def shift(array, axis, step):
    size = lax.axis_size(axis)
    return lax.ppermute(array, axis, [(i, (i + step) % size) for i in range(size)])


def local(latent, routes, gates, up_weight, down_weight):
    block, width = latent.shape
    top = routes.shape[1]
    cores, depth, subs = (lax.axis_size(a) for a in ("core", "z", "sub"))
    experts = depth * cores
    slots = min(block, 3 * block * top // (2 * experts))
    tables = [jnp.swapaxes(up_weight, 1, 2), jnp.swapaxes(down_weight, 1, 2)]
    for step in range(1, cores):
        tables += [shift(tables[0], "core", step), shift(tables[1], "core", step)]
    core = lax.axis_index("core")
    ids = lax.axis_index("z") * cores + (core + cores - jnp.arange(cores, dtype=jnp.int32)) % cores
    ring = [pack(latent, routes, gates, experts)]
    for r in range(1, depth):
        ring.append(shift(ring[-1], "z", 1))
    arrived = [[held] + [shift(held, "sub", s) for s in range(1, subs)] for held in ring]
    home = 0.0
    kinds = [jnp.float32] + [jnp.bfloat16] * (subs - 1)
    for first in range(0, depth, ROUNDS):
        now = range(first, min(depth, first + ROUNDS))
        after = partial[0] if first else ring[min(depth - 1, ROUNDS)]
        partial = run_experts(
            ids, after, sum([arrived[r] for r in now], []), tables, kinds * len(now), block, slots
        )
        for r in now:
            own, *others = partial[(r - first) * subs : (r - first + 1) * subs]
            for s, other in enumerate(others, 1):
                own = own + shift(other, "sub", -s).astype(jnp.float32)
            if r:
                own = shift(own.astype(jnp.bfloat16), "z", -r).astype(jnp.float32)
            home = home + own
    return home.astype(jnp.bfloat16)


def solution(mesh):
    groups, experts, sub = (mesh.shape[a] for a in ("groups", "expert", "sub"))
    inner = Mesh(
        mesh.devices.reshape(groups, experts // CORES, CORES, sub),
        ("groups", "z", "core", "sub"),
    )
    tokens = P(("groups", "z", "core", "sub"), None)
    table = P(("z", "core"), None, "sub")
    return jax.shard_map(
        local,
        mesh=inner,
        in_specs=(tokens, tokens, tokens, table, table),
        out_specs=tokens,
        check_vma=False,
    )
```

```python
import functools
import math

import jax
import jax.numpy as jnp
from jax import lax
from jax.experimental import pallas as pl
from jax.experimental.pallas import tpu as pltpu
from jax.sharding import Mesh, PartitionSpec as P

CORES = 2
TERMS = 3
NT = (((1,), (1,)), ((), ()))
TN = (((0,), (0,)), ((), ()))


def pack_kernel(experts, extra, latent_ref, routes_ref, gates_ref, out_ref):
    block, width = latent_ref.shape
    out_ref[:block, :] = latent_ref[...]
    ids = lax.broadcasted_iota(jnp.int32, (extra, block), 0)
    weight = jnp.zeros((extra, block), jnp.float32)
    for k in range(routes_ref.shape[0]):
        weight = weight + jnp.where(routes_ref[k : k + 1, :] == ids, gates_ref[k : k + 1, :], 0.0)
    out_ref[block:, :] = jnp.zeros((extra, width), jnp.bfloat16)
    for t in range(TERMS):
        term = weight.astype(jnp.bfloat16)
        out_ref[block:, t * block : (t + 1) * block] = term
        weight = weight - term.astype(jnp.float32)


def pack(latent, routes, gates, experts):
    block, width = latent.shape
    extra = -(-experts // 16) * 16
    return pl.pallas_call(
        functools.partial(pack_kernel, experts, extra),
        out_shape=jax.ShapeDtypeStruct((block + extra, width), jnp.bfloat16),
        in_specs=[pl.BlockSpec(memory_space=pltpu.VMEM)] * 3,
        out_specs=pl.BlockSpec(memory_space=pltpu.VMEM),
    )(latent, routes.T, gates.T)


def stage_kernel(after_ref, *refs):
    number = (len(refs) - 1) // 2
    copies = [
        pltpu.make_async_copy(refs[n], refs[number + n], refs[-1].at[n]) for n in range(number)
    ]
    for copy in copies:
        copy.start()
    for copy in copies:
        copy.wait()


def stage(after, arrays):
    return pl.pallas_call(
        stage_kernel,
        out_shape=[jax.ShapeDtypeStruct(a.shape, a.dtype) for a in arrays],
        in_specs=[pl.BlockSpec(memory_space=pl.ANY)]
        + [pl.BlockSpec(memory_space=pltpu.HBM)] * len(arrays),
        out_specs=[pl.BlockSpec(memory_space=pltpu.VMEM)] * len(arrays),
        scratch_shapes=[pltpu.SemaphoreType.DMA((len(arrays),))],
        compiler_params=pltpu.CompilerParams(vmem_limit_bytes=16 * 1024 * 1024),
    )(after, *arrays)


def expert_kernel(block, slots, unit, number, blocks, waits, ids_ref, *refs):
    refs = refs[waits:]
    x_refs, tables, out_refs = refs[:blocks], refs[blocks : blocks + 2 * number], refs[blocks + 2 * number :]
    extra = x_refs[0].shape[0] - block
    earlier = lax.broadcasted_iota(jnp.int32, (block, block), 0)
    later = lax.broadcasted_iota(jnp.int32, (block, block), 1)
    before = (earlier < later).astype(jnp.bfloat16)
    size = unit * slots
    slot = lax.broadcasted_iota(jnp.int32, (size, block), 0)
    row = lax.broadcasted_iota(jnp.int32, (extra, block), 0)
    gates, ranks = [], []
    for x_ref in x_refs:
        gate = 0.0
        for t in range(TERMS):
            gate = gate + x_ref[block:, t * block : (t + 1) * block].astype(jnp.float32)
        gates.append(gate)
        ranks.append(
            jnp.dot((gate > 0).astype(jnp.bfloat16), before, preferred_element_type=jnp.float32)
        )
    sums = [0.0] * blocks
    for n in range(number):
        up_ref, down_ref = tables[2 * n], tables[2 * n + 1]
        mine = row == ids_ref[n]
        picks, scales, rows = [], [], []
        for u in range(blocks // unit):
            parts = []
            scale = 0.0
            for j in range(unit):
                b = u * unit + j
                weight = jnp.sum(jnp.where(mine, gates[b], 0.0), axis=0, keepdims=True)
                rank = jnp.sum(jnp.where(mine, ranks[b], 0.0), axis=0, keepdims=True)
                here = (slot == rank.astype(jnp.int32) + j * slots) & (weight > 0)
                scale = scale + jnp.sum(jnp.where(here, weight, 0.0), axis=1, keepdims=True)
                parts.append(here.astype(jnp.bfloat16))
            tokens = [x_refs[u * unit + j][:block, :] for j in range(unit)]
            pick = jnp.concatenate(parts, axis=1) if unit > 1 else parts[0]
            token = jnp.concatenate(tokens, axis=0) if unit > 1 else tokens[0]
            rows.append(
                jnp.dot(pick, token, preferred_element_type=jnp.float32).astype(jnp.bfloat16)
            )
            picks.append(parts)
            scales.append(scale)
        picked = jnp.concatenate(rows, axis=0)
        preact = lax.dot_general(picked, up_ref[0], NT, preferred_element_type=jnp.float32)
        active = jnp.square(jnp.maximum(preact, 0.0)).astype(jnp.bfloat16)
        summed = jnp.dot(active, down_ref[0], preferred_element_type=jnp.float32)
        for u in range(blocks // unit):
            gated = (summed[u * size : (u + 1) * size] * scales[u]).astype(jnp.bfloat16)
            for j in range(unit):
                b = u * unit + j
                sums[b] = sums[b] + lax.dot_general(
                    picks[u][j], gated, TN, preferred_element_type=jnp.float32
                )
    for b in range(blocks):
        out_refs[b][...] = sums[b].astype(out_refs[b].dtype)


def run_experts(ids, after, arrived, tables, kinds, block, slots):
    blocks, number = len(arrived), len(tables) // 2
    hidden, width = tables[0].shape[1:]
    unit = 16 // math.gcd(16, slots)
    whole = pl.BlockSpec(memory_space=pltpu.VMEM)
    return pl.pallas_call(
        functools.partial(expert_kernel, block, slots, unit, number, blocks, len(after)),
        out_shape=[jax.ShapeDtypeStruct((block, width), kind) for kind in kinds],
        in_specs=[pl.BlockSpec(memory_space=pltpu.SMEM)]
        + [pl.BlockSpec(memory_space=pl.ANY)] * len(after)
        + [whole] * (blocks + len(tables)),
        out_specs=[whole] * blocks,
        compiler_params=pltpu.CompilerParams(vmem_limit_bytes=30 * 1024 * 1024),
        cost_estimate=pl.CostEstimate(
            flops=4 * number * blocks * slots * width * (hidden + block),
            bytes_accessed=5 * blocks * block * width + 2 * len(tables) * width * hidden,
            transcendentals=0,
        ),
    )(ids, *after, *arrived, *tables)


def shift(array, axis, step):
    size = lax.axis_size(axis)
    return lax.ppermute(array, axis, [(i, (i + step) % size) for i in range(size)])


def local(latent, routes, gates, up_weight, down_weight):
    block, width = latent.shape
    top = routes.shape[1]
    cores, depth, subs = (lax.axis_size(a) for a in ("core", "z", "sub"))
    experts = depth * cores
    slots = min(block, 3 * block * top // (2 * experts))
    own = [jnp.swapaxes(up_weight, 1, 2), jnp.swapaxes(down_weight, 1, 2)]
    moved = [shift(table, "core", step) for step in range(1, cores) for table in own]
    core = lax.axis_index("core")
    ids = lax.axis_index("z") * cores + (core + cores - jnp.arange(cores, dtype=jnp.int32)) % cores
    ring = [pack(latent, routes, gates, experts)]
    tables = [*stage(ring[0], own), *moved]
    ring.append(shift(ring[0], "z", 1))
    home = 0.0
    kinds = [jnp.float32] + [jnp.bfloat16] * (subs - 1)
    partial, summed, back = [], [], []
    for r in range(depth):
        arrived = [ring[r]] + [shift(ring[r], "sub", s) for s in range(1, subs)]
        after = [ring[min(r + 1, depth - 1)], *partial[:1], *summed[1:][r - 3 : r - 2]]
        partial = list(run_experts(ids, after, arrived, tables, kinds, block, slots))
        if r + 2 < depth:
            held, partial[0] = lax.optimization_barrier((shift(ring[-1], "z", 1), partial[0]))
            ring.append(held)
        total = partial[0]
        for s in range(1, subs):
            other = shift(partial[s], "sub", -s)
            if r > 1 and s == 1:
                other, back[r - 2] = lax.optimization_barrier((other, back[r - 2]))
            total = total + other.astype(jnp.float32)
        summed.append(total.astype(jnp.bfloat16))
        back.append(shift(summed[r], "z", -r) if r else total)
    for part in back:
        home = home + part.astype(jnp.float32)
    return home.astype(jnp.bfloat16)


def solution(mesh):
    groups, experts, sub = (mesh.shape[a] for a in ("groups", "expert", "sub"))
    inner = Mesh(
        mesh.devices.reshape(groups, experts // CORES, CORES, sub),
        ("groups", "z", "core", "sub"),
    )
    tokens = P(("groups", "z", "core", "sub"), None)
    table = P(("z", "core"), None, "sub")
    return jax.shard_map(
        local,
        mesh=inner,
        in_specs=(tokens, tokens, tokens, table, table),
        out_specs=tokens,
        check_vma=False,
    )
```

```python
import functools
import math

import jax
import jax.numpy as jnp
from jax import lax
from jax.experimental import pallas as pl
from jax.experimental.pallas import tpu as pltpu
from jax.sharding import Mesh, PartitionSpec as P

CORES = 2
TERMS = 3
NT = (((1,), (1,)), ((), ()))
TN = (((0,), (0,)), ((), ()))


def pack_kernel(experts, extra, latent_ref, routes_ref, gates_ref, out_ref):
    block, width = latent_ref.shape
    out_ref[:block, :] = latent_ref[...]
    ids = lax.broadcasted_iota(jnp.int32, (extra, block), 0)
    weight = jnp.zeros((extra, block), jnp.float32)
    for k in range(routes_ref.shape[0]):
        weight = weight + jnp.where(routes_ref[k : k + 1, :] == ids, gates_ref[k : k + 1, :], 0.0)
    out_ref[block:, :] = jnp.zeros((extra, width), jnp.bfloat16)
    for t in range(TERMS):
        term = weight.astype(jnp.bfloat16)
        out_ref[block:, t * block : (t + 1) * block] = term
        weight = weight - term.astype(jnp.float32)


def pack(latent, routes, gates, experts):
    block, width = latent.shape
    extra = -(-experts // 16) * 16
    return pl.pallas_call(
        functools.partial(pack_kernel, experts, extra),
        out_shape=jax.ShapeDtypeStruct((block + extra, width), jnp.bfloat16),
        in_specs=[pl.BlockSpec(memory_space=pltpu.VMEM)] * 3,
        out_specs=pl.BlockSpec(memory_space=pltpu.VMEM),
    )(latent, routes.T, gates.T)


def stage_kernel(after_ref, *refs):
    number = (len(refs) - 1) // 2
    copies = [
        pltpu.make_async_copy(refs[n], refs[number + n], refs[-1].at[n]) for n in range(number)
    ]
    for copy in copies:
        copy.start()
    for copy in copies:
        copy.wait()


def stage(after, arrays):
    return pl.pallas_call(
        stage_kernel,
        out_shape=[jax.ShapeDtypeStruct(a.shape, a.dtype) for a in arrays],
        in_specs=[pl.BlockSpec(memory_space=pl.ANY)]
        + [pl.BlockSpec(memory_space=pltpu.HBM)] * len(arrays),
        out_specs=[pl.BlockSpec(memory_space=pltpu.VMEM)] * len(arrays),
        scratch_shapes=[pltpu.SemaphoreType.DMA((len(arrays),))],
        compiler_params=pltpu.CompilerParams(vmem_limit_bytes=16 * 1024 * 1024),
    )(after, *arrays)


def expert_kernel(block, slots, unit, number, blocks, waits, ids_ref, *refs):
    refs = refs[waits:]
    x_refs, tables, out_refs = refs[:blocks], refs[blocks : blocks + 2 * number], refs[blocks + 2 * number :]
    extra = x_refs[0].shape[0] - block
    earlier = lax.broadcasted_iota(jnp.int32, (block, block), 0)
    later = lax.broadcasted_iota(jnp.int32, (block, block), 1)
    before = (earlier < later).astype(jnp.bfloat16)
    groups = [range(g, min(g + unit, blocks)) for g in range(0, blocks, unit)]
    sizes = [-(-len(g) * slots // 16) * 16 for g in groups]
    row = lax.broadcasted_iota(jnp.int32, (extra, block), 0)
    gates, ranks = [], []
    for x_ref in x_refs:
        gate = 0.0
        for t in range(TERMS):
            gate = gate + x_ref[block:, t * block : (t + 1) * block].astype(jnp.float32)
        gates.append(gate)
        ranks.append(
            jnp.dot((gate > 0).astype(jnp.bfloat16), before, preferred_element_type=jnp.float32)
        )
    sums = [0.0] * blocks
    for n in range(number):
        up_ref, down_ref = tables[2 * n], tables[2 * n + 1]
        mine = row == ids_ref[n]
        picks, scales, rows = [], [], []
        for group, size in zip(groups, sizes):
            slot = lax.broadcasted_iota(jnp.int32, (size, block), 0)
            parts = []
            scale = 0.0
            for j, b in enumerate(group):
                weight = jnp.sum(jnp.where(mine, gates[b], 0.0), axis=0, keepdims=True)
                rank = jnp.sum(jnp.where(mine, ranks[b], 0.0), axis=0, keepdims=True)
                here = (slot == rank.astype(jnp.int32) + j * slots) & (weight > 0)
                scale = scale + jnp.sum(jnp.where(here, weight, 0.0), axis=1, keepdims=True)
                parts.append(here.astype(jnp.bfloat16))
            tokens = [x_refs[b][:block, :] for b in group]
            pick = jnp.concatenate(parts, axis=1) if len(group) > 1 else parts[0]
            token = jnp.concatenate(tokens, axis=0) if len(group) > 1 else tokens[0]
            rows.append(
                jnp.dot(pick, token, preferred_element_type=jnp.float32).astype(jnp.bfloat16)
            )
            picks.append(parts)
            scales.append(scale)
        picked = jnp.concatenate(rows, axis=0) if len(rows) > 1 else rows[0]
        preact = lax.dot_general(picked, up_ref[0], NT, preferred_element_type=jnp.float32)
        active = jnp.square(jnp.maximum(preact, 0.0)).astype(jnp.bfloat16)
        summed = jnp.dot(active, down_ref[0], preferred_element_type=jnp.float32)
        start = 0
        for g, (group, size) in enumerate(zip(groups, sizes)):
            gated = (summed[start : start + size] * scales[g]).astype(jnp.bfloat16)
            start += size
            for j, b in enumerate(group):
                sums[b] = sums[b] + lax.dot_general(
                    picks[g][j], gated, TN, preferred_element_type=jnp.float32
                )
    for b in range(blocks):
        out_refs[b][...] = sums[b].astype(out_refs[b].dtype)


def run_experts(ids, after, arrived, tables, kinds, block, slots):
    blocks, number = len(arrived), len(tables) // 2
    hidden, width = tables[0].shape[1:]
    unit = 16 // math.gcd(16, slots)
    whole = pl.BlockSpec(memory_space=pltpu.VMEM)
    return pl.pallas_call(
        functools.partial(expert_kernel, block, slots, unit, number, blocks, len(after)),
        out_shape=[jax.ShapeDtypeStruct((block, width), kind) for kind in kinds],
        in_specs=[pl.BlockSpec(memory_space=pltpu.SMEM)]
        + [pl.BlockSpec(memory_space=pl.ANY)] * len(after)
        + [whole] * (blocks + len(tables)),
        out_specs=[whole] * blocks,
        compiler_params=pltpu.CompilerParams(vmem_limit_bytes=30 * 1024 * 1024),
        cost_estimate=pl.CostEstimate(
            flops=4 * number * blocks * slots * width * (hidden + block),
            bytes_accessed=5 * blocks * block * width + 2 * len(tables) * width * hidden,
            transcendentals=0,
        ),
    )(ids, *after, *arrived, *tables)


def shift(array, axis, step):
    size = lax.axis_size(axis)
    return lax.ppermute(array, axis, [(i, (i + step) % size) for i in range(size)])


def follow(array, first):
    return lax.optimization_barrier((array, first))[0]


def shift_both(array, outer, step, inner, turn):
    sizes = lax.axis_size(outer), lax.axis_size(inner)
    pairs = [
        (i * sizes[1] + k, (i + step) % sizes[0] * sizes[1] + (k + turn) % sizes[1])
        for i in range(sizes[0])
        for k in range(sizes[1])
    ]
    return lax.ppermute(array, (outer, inner), pairs)


def local(latent, routes, gates, up_weight, down_weight):
    block, width = latent.shape
    top = routes.shape[1]
    cores, depth, subs = (lax.axis_size(a) for a in ("core", "z", "sub"))
    experts = depth * cores
    slots = min(block, 3 * block * top // (2 * experts))
    own = [jnp.swapaxes(up_weight, 1, 2), jnp.swapaxes(down_weight, 1, 2)]
    moved = [shift(table, "core", step) for step in range(1, cores) for table in own]
    core = lax.axis_index("core")
    ids = lax.axis_index("z") * cores + (core + cores - jnp.arange(cores, dtype=jnp.int32)) % cores
    ring = [pack(latent, routes, gates, experts)]
    tables = [*stage(ring[0], own), *moved]
    ring.append(follow(shift(ring[0], "z", 1), tables[0]))
    last = depth - 1
    kept = [None] * depth
    others, totals = [], {}
    after = []

    def total(j, behind=None):
        rows = kept[j]
        for s, other in enumerate(others[j], 1):
            other = shift(other, "sub", -s)
            if behind is not None:
                other = follow(other, behind)
            rows = rows + other.astype(jnp.float32)
        return rows.astype(jnp.bfloat16) if j else rows

    for j in range(depth):
        handed = [shift(ring[j], "sub", s) for s in range(1, subs)]
        fresh = ([0] if j == 0 else []) + [j + 1] * (j < last)
        kinds = [jnp.bfloat16] * len(handed)
        kinds += [jnp.bfloat16 if r == last else jnp.float32 for r in fresh]
        if j > 2:
            totals[j - 2] = total(j - 2, after[0])
            after.append(totals[j - 2])
        partial = run_experts(
            ids, after, handed + [ring[r] for r in fresh], tables, kinds, block, slots
        )
        after = [partial[0]]
        if j + 2 < depth:
            ring.append(follow(shift(ring[-1], "z", 1), partial[0]))
        for r, rows in zip(fresh, partial[subs - 1 :]):
            kept[r] = rows
        others.append(partial[: subs - 1])
    corner = [shift_both(other, "z", -last, "sub", -s) for s, other in enumerate(others[last], 1)]
    others[0] = [follow(other, others[last][0]) for other in others[0]]
    for j in range(last):
        if j not in totals:
            totals[j] = total(j, others[last][0])
    back = [shift(kept[last], "z", -last)] + [shift(totals[j], "z", -j) for j in range(1, last)]
    late = back.pop()
    home = sum(rows.astype(jnp.float32) for rows in back)
    home, *corner = lax.optimization_barrier((home, *corner))
    home = home + totals[0] + sum(rows.astype(jnp.float32) for rows in corner)
    home, late = lax.optimization_barrier((home, late))
    home = home + late.astype(jnp.float32)
    return home.astype(jnp.bfloat16)


def solution(mesh):
    groups, experts, sub = (mesh.shape[a] for a in ("groups", "expert", "sub"))
    inner = Mesh(
        mesh.devices.reshape(groups, experts // CORES, CORES, sub),
        ("groups", "z", "core", "sub"),
    )
    tokens = P(("groups", "z", "core", "sub"), None)
    table = P(("z", "core"), None, "sub")
    return jax.shard_map(
        local,
        mesh=inner,
        in_specs=(tokens, tokens, tokens, table, table),
        out_specs=tokens,
        check_vma=False,
    )
```

```python
import functools
import math

import jax
import jax.numpy as jnp
from jax import lax
from jax.experimental import pallas as pl
from jax.experimental.pallas import tpu as pltpu
from jax.sharding import Mesh, PartitionSpec as P

CORES = 2
TERMS = 3
NT = (((1,), (1,)), ((), ()))
TN = (((0,), (0,)), ((), ()))


def pack_kernel(experts, extra, latent_ref, routes_ref, gates_ref, out_ref):
    block, width = latent_ref.shape
    out_ref[:block, :] = latent_ref[...]
    ids = lax.broadcasted_iota(jnp.int32, (extra, block), 0)
    weight = jnp.zeros((extra, block), jnp.float32)
    for k in range(routes_ref.shape[0]):
        weight = weight + jnp.where(routes_ref[k : k + 1, :] == ids, gates_ref[k : k + 1, :], 0.0)
    out_ref[block:, :] = jnp.zeros((extra, width), jnp.bfloat16)
    for t in range(TERMS):
        term = weight.astype(jnp.bfloat16)
        out_ref[block:, t * block : (t + 1) * block] = term
        weight = weight - term.astype(jnp.float32)


def pack(latent, routes, gates, experts):
    block, width = latent.shape
    extra = -(-experts // 16) * 16
    return pl.pallas_call(
        functools.partial(pack_kernel, experts, extra),
        out_shape=jax.ShapeDtypeStruct((block + extra, width), jnp.bfloat16),
        in_specs=[pl.BlockSpec(memory_space=pltpu.VMEM)] * 3,
        out_specs=pl.BlockSpec(memory_space=pltpu.VMEM),
        compiler_params=pltpu.CompilerParams(vmem_limit_bytes=4 * 1024 * 1024),
    )(latent, routes.T, gates.T)


def stage_kernel(after_ref, *refs):
    number = (len(refs) - 1) // 2
    copies = [
        pltpu.make_async_copy(refs[n], refs[number + n], refs[-1].at[n]) for n in range(number)
    ]
    for copy in copies:
        copy.start()
    for copy in copies:
        copy.wait()


def stage(after, arrays):
    return pl.pallas_call(
        stage_kernel,
        out_shape=[jax.ShapeDtypeStruct(a.shape, a.dtype) for a in arrays],
        in_specs=[pl.BlockSpec(memory_space=pl.ANY)]
        + [pl.BlockSpec(memory_space=pltpu.HBM)] * len(arrays),
        out_specs=[pl.BlockSpec(memory_space=pltpu.VMEM)] * len(arrays),
        scratch_shapes=[pltpu.SemaphoreType.DMA((len(arrays),))],
        compiler_params=pltpu.CompilerParams(vmem_limit_bytes=16 * 1024 * 1024),
    )(after, *arrays)


def expert_kernel(block, slots, unit, number, blocks, waits, *refs):
    first, core = lax.axis_index("z") * number, lax.axis_index("core")
    refs = refs[waits:]
    x_refs, tables, out_refs = refs[:blocks], refs[blocks : blocks + 2 * number], refs[blocks + 2 * number :]
    extra = x_refs[0].shape[0] - block
    earlier = lax.broadcasted_iota(jnp.int32, (block, block), 0)
    later = lax.broadcasted_iota(jnp.int32, (block, block), 1)
    before = (earlier < later).astype(jnp.bfloat16)
    groups = [range(g, min(g + unit, blocks)) for g in range(0, blocks, unit)]
    sizes = [-(-len(g) * slots // 16) * 16 for g in groups]
    row = lax.broadcasted_iota(jnp.int32, (extra, block), 0)
    gates, ranks = [], []
    for x_ref in x_refs:
        gate = 0.0
        for t in range(TERMS):
            gate = gate + x_ref[block:, t * block : (t + 1) * block].astype(jnp.float32)
        gates.append(gate)
        ranks.append(
            jnp.dot((gate > 0).astype(jnp.bfloat16), before, preferred_element_type=jnp.float32)
        )
    sums = [0.0] * blocks
    for n in range(number):
        up_ref, down_ref = tables[2 * n], tables[2 * n + 1]
        mine = row == first + lax.rem(core + number - n, number)
        picks, scales, rows = [], [], []
        for group, size in zip(groups, sizes):
            slot = lax.broadcasted_iota(jnp.int32, (size, block), 0)
            parts = []
            scale = 0.0
            for j, b in enumerate(group):
                weight = jnp.sum(jnp.where(mine, gates[b], 0.0), axis=0, keepdims=True)
                rank = jnp.sum(jnp.where(mine, ranks[b], 0.0), axis=0, keepdims=True)
                here = (slot == rank.astype(jnp.int32) + j * slots) & (weight > 0)
                scale = scale + jnp.sum(jnp.where(here, weight, 0.0), axis=1, keepdims=True)
                parts.append(here.astype(jnp.bfloat16))
            tokens = [x_refs[b][:block, :] for b in group]
            pick = jnp.concatenate(parts, axis=1) if len(group) > 1 else parts[0]
            token = jnp.concatenate(tokens, axis=0) if len(group) > 1 else tokens[0]
            rows.append(
                jnp.dot(pick, token, preferred_element_type=jnp.float32).astype(jnp.bfloat16)
            )
            picks.append(parts)
            scales.append(scale)
        picked = jnp.concatenate(rows, axis=0) if len(rows) > 1 else rows[0]
        preact = lax.dot_general(picked, up_ref[0], NT, preferred_element_type=jnp.float32)
        active = jnp.square(jnp.maximum(preact, 0.0)).astype(jnp.bfloat16)
        summed = jnp.dot(active, down_ref[0], preferred_element_type=jnp.float32)
        start = 0
        for g, (group, size) in enumerate(zip(groups, sizes)):
            gated = (summed[start : start + size] * scales[g]).astype(jnp.bfloat16)
            start += size
            for j, b in enumerate(group):
                sums[b] = sums[b] + lax.dot_general(
                    picks[g][j], gated, TN, preferred_element_type=jnp.float32
                )
    for b in range(blocks):
        out_refs[b][...] = sums[b].astype(out_refs[b].dtype)


def run_experts(after, arrived, tables, kinds, block, slots):
    blocks, number = len(arrived), len(tables) // 2
    hidden, width = tables[0].shape[1:]
    unit = 16 // math.gcd(16, slots)
    whole = pl.BlockSpec(memory_space=pltpu.VMEM)
    return pl.pallas_call(
        functools.partial(expert_kernel, block, slots, unit, number, blocks, len(after)),
        out_shape=[jax.ShapeDtypeStruct((block, width), kind) for kind in kinds],
        in_specs=[pl.BlockSpec(memory_space=pl.ANY)] * len(after)
        + [whole] * (blocks + len(tables)),
        out_specs=[whole] * blocks,
        compiler_params=pltpu.CompilerParams(vmem_limit_bytes=30 * 1024 * 1024),
        cost_estimate=pl.CostEstimate(
            flops=4 * number * blocks * slots * width * (hidden + block),
            bytes_accessed=5 * blocks * block * width + 2 * len(tables) * width * hidden,
            transcendentals=0,
        ),
    )(*after, *arrived, *tables)


def shift(array, axis, step):
    size = lax.axis_size(axis)
    return lax.ppermute(array, axis, [(i, (i + step) % size) for i in range(size)])


def follow(array, first):
    return lax.optimization_barrier((array, first))[0]


def shift_both(array, outer, step, inner, turn):
    sizes = lax.axis_size(outer), lax.axis_size(inner)
    pairs = [
        (i * sizes[1] + k, (i + step) % sizes[0] * sizes[1] + (k + turn) % sizes[1])
        for i in range(sizes[0])
        for k in range(sizes[1])
    ]
    return lax.ppermute(array, (outer, inner), pairs)


def local(latent, routes, gates, up_weight, down_weight):
    block, width = latent.shape
    top = routes.shape[1]
    cores, depth, subs = (lax.axis_size(a) for a in ("core", "z", "sub"))
    experts = depth * cores
    slots = min(block, 3 * block * top // (2 * experts))
    own = [jnp.swapaxes(up_weight, 1, 2), jnp.swapaxes(down_weight, 1, 2)]
    moved = [shift(table, "core", step) for step in range(1, cores) for table in own]
    ring = [pack(latent, routes, gates, experts)]
    tables = [*stage(ring[0], own), *moved]
    ring.append(follow(shift(ring[0], "z", 1), tables[0]))
    last = depth - 1
    kept = [None] * depth
    others, totals = [], {}
    after = []

    def total(j, behind=None):
        rows = kept[j]
        for s, other in enumerate(others[j], 1):
            other = shift(other, "sub", -s)
            if behind is not None:
                other = follow(other, behind)
            rows = rows + other.astype(jnp.float32)
        return rows.astype(jnp.bfloat16) if j else rows

    for j in range(depth):
        handed = [shift(ring[j], "sub", s) for s in range(1, subs)]
        fresh = ([0] if j == 0 else []) + [j + 1] * (j < last)
        kinds = [jnp.bfloat16] * len(handed)
        kinds += [jnp.bfloat16 if r == last else jnp.float32 for r in fresh]
        if j > 2:
            totals[j - 2] = total(j - 2, after[0])
            after.append(totals[j - 2])
        partial = run_experts(
            after, handed + [ring[r] for r in fresh], tables, kinds, block, slots
        )
        after = [partial[0]]
        if j + 2 < depth:
            ring.append(follow(shift(ring[-1], "z", 1), partial[0]))
        for r, rows in zip(fresh, partial[subs - 1 :]):
            kept[r] = rows
        others.append(partial[: subs - 1])
    corner = [shift_both(other, "z", -last, "sub", -s) for s, other in enumerate(others[last], 1)]
    others[0] = [follow(other, others[last][0]) for other in others[0]]
    for j in range(last):
        if j not in totals:
            totals[j] = total(j, others[last][0])
    back = [shift(kept[last], "z", -last)] + [shift(totals[j], "z", -j) for j in range(1, last)]
    late = back.pop()
    home = sum(rows.astype(jnp.float32) for rows in back)
    home, *corner = lax.optimization_barrier((home, *corner))
    home = home + totals[0] + sum(rows.astype(jnp.float32) for rows in corner)
    home, late = lax.optimization_barrier((home, late))
    home = home + late.astype(jnp.float32)
    return home.astype(jnp.bfloat16)


def solution(mesh):
    groups, experts, sub = (mesh.shape[a] for a in ("groups", "expert", "sub"))
    inner = Mesh(
        mesh.devices.reshape(groups, experts // CORES, CORES, sub),
        ("groups", "z", "core", "sub"),
    )
    tokens = P(("groups", "z", "core", "sub"), None)
    table = P(("z", "core"), None, "sub")
    return jax.shard_map(
        local,
        mesh=inner,
        in_specs=(tokens, tokens, tokens, table, table),
        out_specs=tokens,
        check_vma=False,
    )
```

```python
import functools
import math

import jax
import jax.numpy as jnp
from jax import lax
from jax.experimental import pallas as pl
from jax.experimental.pallas import tpu as pltpu
from jax.sharding import Mesh, PartitionSpec as P

CORES = 2
TERMS = 3
NT = (((1,), (1,)), ((), ()))
TN = (((0,), (0,)), ((), ()))


def pack_kernel(experts, extra, latent_ref, routes_ref, gates_ref, out_ref):
    block, width = latent_ref.shape
    out_ref[:block, :] = latent_ref[...]
    ids = lax.broadcasted_iota(jnp.int32, (extra, block), 0)
    weight = jnp.zeros((extra, block), jnp.float32)
    for k in range(routes_ref.shape[0]):
        weight = weight + jnp.where(routes_ref[k : k + 1, :] == ids, gates_ref[k : k + 1, :], 0.0)
    out_ref[block:, :] = jnp.zeros((extra, width), jnp.bfloat16)
    for t in range(TERMS):
        term = weight.astype(jnp.bfloat16)
        out_ref[block:, t * block : (t + 1) * block] = term
        weight = weight - term.astype(jnp.float32)


def pack(latent, routes, gates, experts):
    block, width = latent.shape
    extra = -(-experts // 16) * 16
    return pl.pallas_call(
        functools.partial(pack_kernel, experts, extra),
        out_shape=jax.ShapeDtypeStruct((block + extra, width), jnp.bfloat16),
        in_specs=[pl.BlockSpec(memory_space=pltpu.VMEM)] * 3,
        out_specs=pl.BlockSpec(memory_space=pltpu.VMEM),
        compiler_params=pltpu.CompilerParams(vmem_limit_bytes=4 * 1024 * 1024),
    )(latent, routes.T, gates.T)


def stage_kernel(after_ref, *refs):
    number = (len(refs) - 1) // 2
    copies = [
        pltpu.make_async_copy(refs[n], refs[number + n], refs[-1].at[n]) for n in range(number)
    ]
    for copy in copies:
        copy.start()
    for copy in copies:
        copy.wait()


def stage(after, arrays):
    return pl.pallas_call(
        stage_kernel,
        out_shape=[jax.ShapeDtypeStruct(a.shape, a.dtype) for a in arrays],
        in_specs=[pl.BlockSpec(memory_space=pl.ANY)]
        + [pl.BlockSpec(memory_space=pltpu.HBM)] * len(arrays),
        out_specs=[pl.BlockSpec(memory_space=pltpu.VMEM)] * len(arrays),
        scratch_shapes=[pltpu.SemaphoreType.DMA((len(arrays),))],
        compiler_params=pltpu.CompilerParams(vmem_limit_bytes=16 * 1024 * 1024),
    )(after, *arrays)


def expert_kernel(block, slots, unit, number, blocks, waits, *refs):
    first, core = lax.axis_index("z") * number, lax.axis_index("core")
    refs = refs[waits:]
    x_refs, tables, out_refs = refs[:blocks], refs[blocks : blocks + 2 * number], refs[blocks + 2 * number :]
    extra = x_refs[0].shape[0] - block
    earlier = lax.broadcasted_iota(jnp.int32, (block, block), 0)
    later = lax.broadcasted_iota(jnp.int32, (block, block), 1)
    before = (earlier < later).astype(jnp.bfloat16)
    groups = [range(g, min(g + unit, blocks)) for g in range(0, blocks, unit)]
    sizes = [-(-len(g) * slots // 16) * 16 for g in groups]
    row = lax.broadcasted_iota(jnp.int32, (extra, block), 0)
    gates, ranks = [], []
    for x_ref in x_refs:
        gate = 0.0
        for t in range(TERMS):
            gate = gate + x_ref[block:, t * block : (t + 1) * block].astype(jnp.float32)
        gates.append(gate)
        ranks.append(
            jnp.dot((gate > 0).astype(jnp.bfloat16), before, preferred_element_type=jnp.float32)
        )
    sums = [0.0] * blocks
    for n in range(number):
        up_ref, down_ref = tables[2 * n], tables[2 * n + 1]
        mine = row == first + lax.rem(core + number - n, number)
        picks, scales, rows = [], [], []
        for group, size in zip(groups, sizes):
            slot = lax.broadcasted_iota(jnp.int32, (size, block), 0)
            parts = []
            scale = 0.0
            for j, b in enumerate(group):
                weight = jnp.sum(jnp.where(mine, gates[b], 0.0), axis=0, keepdims=True)
                rank = jnp.sum(jnp.where(mine, ranks[b], 0.0), axis=0, keepdims=True)
                here = (slot == rank.astype(jnp.int32) + j * slots) & (weight > 0)
                scale = scale + jnp.sum(jnp.where(here, weight, 0.0), axis=1, keepdims=True)
                parts.append(here.astype(jnp.bfloat16))
            tokens = [x_refs[b][:block, :] for b in group]
            pick = jnp.concatenate(parts, axis=1) if len(group) > 1 else parts[0]
            token = jnp.concatenate(tokens, axis=0) if len(group) > 1 else tokens[0]
            rows.append(
                jnp.dot(pick, token, preferred_element_type=jnp.float32).astype(jnp.bfloat16)
            )
            picks.append(parts)
            scales.append(scale)
        picked = jnp.concatenate(rows, axis=0) if len(rows) > 1 else rows[0]
        preact = lax.dot_general(picked, up_ref[0], NT, preferred_element_type=jnp.float32)
        active = jnp.square(jnp.maximum(preact, 0.0)).astype(jnp.bfloat16)
        summed = jnp.dot(active, down_ref[0], preferred_element_type=jnp.float32)
        start = 0
        for g, (group, size) in enumerate(zip(groups, sizes)):
            gated = (summed[start : start + size] * scales[g]).astype(jnp.bfloat16)
            start += size
            for j, b in enumerate(group):
                sums[b] = sums[b] + lax.dot_general(
                    picks[g][j], gated, TN, preferred_element_type=jnp.float32
                )
    for b in range(blocks):
        out_refs[b][...] = sums[b].astype(out_refs[b].dtype)


def run_experts(after, arrived, tables, kinds, block, slots):
    blocks, number = len(arrived), len(tables) // 2
    hidden, width = tables[0].shape[1:]
    unit = 16 // math.gcd(16, slots)
    whole = pl.BlockSpec(memory_space=pltpu.VMEM)
    return pl.pallas_call(
        functools.partial(expert_kernel, block, slots, unit, number, blocks, len(after)),
        out_shape=[jax.ShapeDtypeStruct((block, width), kind) for kind in kinds],
        in_specs=[pl.BlockSpec(memory_space=pl.ANY)] * len(after)
        + [whole] * (blocks + len(tables)),
        out_specs=[whole] * blocks,
        compiler_params=pltpu.CompilerParams(vmem_limit_bytes=30 * 1024 * 1024),
        cost_estimate=pl.CostEstimate(
            flops=4 * number * blocks * slots * width * (hidden + block),
            bytes_accessed=5 * blocks * block * width + 2 * len(tables) * width * hidden,
            transcendentals=0,
        ),
    )(*after, *arrived, *tables)


def shift(array, axis, step):
    size = lax.axis_size(axis)
    return lax.ppermute(array, axis, [(i, (i + step) % size) for i in range(size)])


def follow(array, first):
    return lax.optimization_barrier((array, first))[0]


def arrival_order(depth):
    ahead, behind = list(range(2, depth // 2 + 1)), list(range(depth - 1, depth // 2, -1))
    order = list(range(min(depth, 2)))
    while ahead or behind:
        order += ahead[:1] + [r for r in behind[:1] if r > 1]
        ahead, behind = ahead[1:], behind[1:]
    return order


def local(latent, routes, gates, up_weight, down_weight):
    block, width = latent.shape
    top = routes.shape[1]
    cores, depth, subs = (lax.axis_size(a) for a in ("core", "z", "sub"))
    experts = depth * cores
    slots = min(block, 3 * block * top // (2 * experts))
    own = [jnp.swapaxes(up_weight, 1, 2), jnp.swapaxes(down_weight, 1, 2)]
    moved = [shift(table, "core", step) for step in range(1, cores) for table in own]
    ring = {0: pack(latent, routes, gates, experts)}
    tables = [*stage(ring[0], own), *moved]
    turns = arrival_order(depth)
    ring[1] = follow(shift(ring[0], "z", 1), tables[0])
    kept, others, totals = {}, {}, {}
    firsts = []

    def fetch(p):
        r = turns[p]
        held = shift(ring[r - 1], "z", 1) if r <= depth // 2 else shift(ring[(r + 1) % depth], "z", -1)
        ring[r] = follow(held, firsts[-1])

    def total(r, behind):
        rows = kept[r]
        for s, other in enumerate(others[r], 1):
            rows = rows + follow(shift(other, "sub", -s), behind).astype(jnp.float32)
        return rows

    def send_home(order, step):
        passing = None
        for r in order:
            rows = totals[r] if passing is None else totals[r] + passing.astype(jnp.float32)
            leaving = rows.astype(jnp.bfloat16)
            passing = shift(leaving, "z", step)
        return leaving, passing

    for p, r in enumerate(turns):
        handed = [shift(ring[r], "sub", s) for s in range(1, subs)]
        fresh = turns[:2] if p == 0 else turns[p + 1 : p + 2]
        kinds = [jnp.bfloat16] * len(handed) + [jnp.float32] * len(fresh)
        after = firsts[-1:] + ([ring[turns[p + 2]]] if 0 < p < depth - 2 else [])
        if p > 2:
            early = turns[p - 2]
            totals[early] = total(early, firsts[-1])
            after.append(totals[early])
        partial = run_experts(after, handed + [ring[f] for f in fresh], tables, kinds, block, slots)
        firsts.append(partial[0])
        for q in (2, 3) if p == 0 else (p + 3,):
            if q < depth:
                fetch(q)
        for f, rows in zip(fresh, partial[subs - 1 :]):
            kept[f] = rows
        others[r] = partial[: subs - 1]
    for r in turns[1:]:
        if r not in totals:
            totals[r] = total(r, others[turns[-1]][0])
    homeward = [send_home(range(depth - 1, depth // 2, -1)[::-1], 1)] if depth > 2 else []
    homeward.append(send_home(range(depth // 2, 0, -1), -1))
    others[0] = [follow(other, homeward[0][0]) for other in others[0]]
    home = total(0, homeward[0][0])
    for _, rows in homeward:
        home = home + rows.astype(jnp.float32)
    return home.astype(jnp.bfloat16)


def solution(mesh):
    groups, experts, sub = (mesh.shape[a] for a in ("groups", "expert", "sub"))
    inner = Mesh(
        mesh.devices.reshape(groups, experts // CORES, CORES, sub),
        ("groups", "z", "core", "sub"),
    )
    tokens = P(("groups", "z", "core", "sub"), None)
    table = P(("z", "core"), None, "sub")
    return jax.shard_map(
        local,
        mesh=inner,
        in_specs=(tokens, tokens, tokens, table, table),
        out_specs=tokens,
        check_vma=False,
    )
```

```python
import functools
import math

import jax
import jax.numpy as jnp
from jax import lax
from jax.experimental import pallas as pl
from jax.experimental.pallas import tpu as pltpu
from jax.sharding import Mesh, PartitionSpec as P

CORES = 2
TERMS = 3
NT = (((1,), (1,)), ((), ()))
TN = (((0,), (0,)), ((), ()))


def pack_kernel(experts, extra, latent_ref, routes_ref, gates_ref, out_ref):
    block, width = latent_ref.shape
    out_ref[:block, :] = latent_ref[...]
    ids = lax.broadcasted_iota(jnp.int32, (extra, block), 0)
    weight = jnp.zeros((extra, block), jnp.float32)
    for k in range(routes_ref.shape[0]):
        weight = weight + jnp.where(routes_ref[k : k + 1, :] == ids, gates_ref[k : k + 1, :], 0.0)
    out_ref[block:, :] = jnp.zeros((extra, width), jnp.bfloat16)
    for t in range(TERMS):
        term = weight.astype(jnp.bfloat16)
        out_ref[block:, t * block : (t + 1) * block] = term
        weight = weight - term.astype(jnp.float32)


def pack(latent, routes, gates, experts):
    block, width = latent.shape
    extra = -(-experts // 16) * 16
    return pl.pallas_call(
        functools.partial(pack_kernel, experts, extra),
        out_shape=jax.ShapeDtypeStruct((block + extra, width), jnp.bfloat16),
        in_specs=[pl.BlockSpec(memory_space=pltpu.VMEM)] * 3,
        out_specs=pl.BlockSpec(memory_space=pltpu.VMEM),
        compiler_params=pltpu.CompilerParams(vmem_limit_bytes=4 * 1024 * 1024),
    )(latent, routes.T, gates.T)


def stage_kernel(after_ref, *refs):
    number = (len(refs) - 1) // 2
    copies = [
        pltpu.make_async_copy(refs[n], refs[number + n], refs[-1].at[n]) for n in range(number)
    ]
    for copy in copies:
        copy.start()
    for copy in copies:
        copy.wait()


def stage(after, arrays):
    return pl.pallas_call(
        stage_kernel,
        out_shape=[jax.ShapeDtypeStruct(a.shape, a.dtype) for a in arrays],
        in_specs=[pl.BlockSpec(memory_space=pl.ANY)]
        + [pl.BlockSpec(memory_space=pltpu.HBM)] * len(arrays),
        out_specs=[pl.BlockSpec(memory_space=pltpu.VMEM)] * len(arrays),
        scratch_shapes=[pltpu.SemaphoreType.DMA((len(arrays),))],
        compiler_params=pltpu.CompilerParams(vmem_limit_bytes=16 * 1024 * 1024),
    )(after, *arrays)


def expert_kernel(block, slots, unit, number, blocks, waits, *refs):
    first, core = lax.axis_index("z") * number, lax.axis_index("core")
    refs = refs[waits:]
    x_refs, tables, out_refs = refs[:blocks], refs[blocks : blocks + 2 * number], refs[blocks + 2 * number :]
    extra = x_refs[0].shape[0] - block
    earlier = lax.broadcasted_iota(jnp.int32, (block, block), 0)
    later = lax.broadcasted_iota(jnp.int32, (block, block), 1)
    before = (earlier < later).astype(jnp.bfloat16)
    groups = [range(g, min(g + unit, blocks)) for g in range(0, blocks, unit)]
    sizes = [-(-len(g) * slots // 16) * 16 for g in groups]
    row = lax.broadcasted_iota(jnp.int32, (extra, block), 0)
    gates, ranks = [], []
    for x_ref in x_refs:
        gate = 0.0
        for t in range(TERMS):
            gate = gate + x_ref[block:, t * block : (t + 1) * block].astype(jnp.float32)
        gates.append(gate)
        ranks.append(
            jnp.dot((gate > 0).astype(jnp.bfloat16), before, preferred_element_type=jnp.float32)
        )
    sums = [0.0] * blocks
    for n in range(number):
        up_ref, down_ref = tables[2 * n], tables[2 * n + 1]
        mine = row == first + lax.rem(core + number - n, number)
        picks, scales, rows = [], [], []
        for group, size in zip(groups, sizes):
            slot = lax.broadcasted_iota(jnp.int32, (size, block), 0)
            parts = []
            scale = 0.0
            for j, b in enumerate(group):
                weight = jnp.sum(jnp.where(mine, gates[b], 0.0), axis=0, keepdims=True)
                rank = jnp.sum(jnp.where(mine, ranks[b], 0.0), axis=0, keepdims=True)
                here = (slot == rank.astype(jnp.int32) + j * slots) & (weight > 0)
                scale = scale + jnp.sum(jnp.where(here, weight, 0.0), axis=1, keepdims=True)
                parts.append(here.astype(jnp.bfloat16))
            tokens = [x_refs[b][:block, :] for b in group]
            pick = jnp.concatenate(parts, axis=1) if len(group) > 1 else parts[0]
            token = jnp.concatenate(tokens, axis=0) if len(group) > 1 else tokens[0]
            rows.append(
                jnp.dot(pick, token, preferred_element_type=jnp.float32).astype(jnp.bfloat16)
            )
            picks.append(parts)
            scales.append(scale)
        picked = jnp.concatenate(rows, axis=0) if len(rows) > 1 else rows[0]
        preact = lax.dot_general(picked, up_ref[0], NT, preferred_element_type=jnp.float32)
        active = jnp.square(jnp.maximum(preact, 0.0)).astype(jnp.bfloat16)
        summed = jnp.dot(active, down_ref[0], preferred_element_type=jnp.float32)
        start = 0
        for g, (group, size) in enumerate(zip(groups, sizes)):
            gated = (summed[start : start + size] * scales[g]).astype(jnp.bfloat16)
            start += size
            for j, b in enumerate(group):
                sums[b] = sums[b] + lax.dot_general(
                    picks[g][j], gated, TN, preferred_element_type=jnp.float32
                )
    for b in range(blocks):
        out_refs[b][...] = sums[b].astype(out_refs[b].dtype)


def run_experts(after, arrived, tables, kinds, block, slots):
    blocks, number = len(arrived), len(tables) // 2
    hidden, width = tables[0].shape[1:]
    unit = 16 // math.gcd(16, slots)
    whole = pl.BlockSpec(memory_space=pltpu.VMEM)
    return pl.pallas_call(
        functools.partial(expert_kernel, block, slots, unit, number, blocks, len(after)),
        out_shape=[jax.ShapeDtypeStruct((block, width), kind) for kind in kinds],
        in_specs=[pl.BlockSpec(memory_space=pl.ANY)] * len(after)
        + [whole] * (blocks + len(tables)),
        out_specs=[whole] * blocks,
        compiler_params=pltpu.CompilerParams(vmem_limit_bytes=30 * 1024 * 1024),
        cost_estimate=pl.CostEstimate(
            flops=4 * number * blocks * slots * width * (hidden + block),
            bytes_accessed=5 * blocks * block * width + 2 * len(tables) * width * hidden,
            transcendentals=0,
        ),
    )(*after, *arrived, *tables)


def shift(array, axis, step):
    size = lax.axis_size(axis)
    return lax.ppermute(array, axis, [(i, (i + step) % size) for i in range(size)])


def follow(array, first):
    return lax.optimization_barrier((array, first))[0]


def local(latent, routes, gates, up_weight, down_weight):
    block, width = latent.shape
    top = routes.shape[1]
    cores, depth, subs = (lax.axis_size(a) for a in ("core", "z", "sub"))
    experts = depth * cores
    slots = min(block, 3 * block * top // (2 * experts))
    own = [jnp.swapaxes(up_weight, 1, 2), jnp.swapaxes(down_weight, 1, 2)]
    moved = [shift(table, "core", step) for step in range(1, cores) for table in own]
    ring = [pack(latent, routes, gates, experts)]
    tables = [*stage(ring[0], own), *moved]
    ring.append(follow(shift(ring[0], "z", 1), tables[0]))
    last = depth - 1
    kept, others = {}, {}
    totals, home = {}, None
    firsts = []

    def total(r, *behind):
        rows = kept[r]
        for s, other in enumerate(others[r], 1):
            other = shift(other, "sub", -s)
            for first in behind:
                other = follow(other, first)
            rows = rows + other.astype(jnp.float32)
        return rows

    for j in range(depth):
        handed = [shift(ring[j], "sub", s) for s in range(1, subs)]
        fresh = ([0] if j == 0 else []) + [j + 1] * (j < last)
        kinds = [jnp.bfloat16] * len(handed)
        kinds += [jnp.bfloat16 if r == 1 else jnp.float32 for r in fresh]
        after = firsts[-1:]
        if j == last and j > 1:
            rows = follow(shift(kept[1], "z", -1), firsts[-1])
            home = kept[0] + rows.astype(jnp.float32)
            after = after + [home]
        if j > 3:
            totals[j - 2] = total(j - 2, firsts[-1]).astype(jnp.bfloat16)
            after = after + [totals[j - 2]]
        partial = run_experts(after, handed + [ring[r] for r in fresh], tables, kinds, block, slots)
        firsts.append(partial[0])
        if j + 2 < depth:
            ring.append(follow(shift(ring[-1], "z", 1), partial[0]))
        for r, rows in zip(fresh, partial[subs - 1 :]):
            kept[r] = rows
        others[j] = partial[: subs - 1]
    if home is None:
        home = kept[0] + sum(shift(kept[r], "z", -r).astype(jnp.float32) for r in range(1, depth))
    joined = others[0]
    if depth > 1:
        joined = [
            (mine.astype(jnp.float32) + shift(rows, "z", -1).astype(jnp.float32)).astype(jnp.bfloat16)
            for mine, rows in zip(others[0], others[1])
        ]
    for r in range(2, depth):
        if r not in totals:
            behind = [firsts[-1]] + (joined if r < last else [])
            totals[r] = total(r, *behind).astype(jnp.bfloat16)
    for s, rows in enumerate(joined, 1):
        if depth > 2:
            rows = follow(rows, totals[last])
        home = home + shift(rows, "sub", -s).astype(jnp.float32)
    for r in range(2, depth):
        home = home + shift(totals[r], "z", -r).astype(jnp.float32)
    return home.astype(jnp.bfloat16)


def solution(mesh):
    groups, experts, sub = (mesh.shape[a] for a in ("groups", "expert", "sub"))
    inner = Mesh(
        mesh.devices.reshape(groups, experts // CORES, CORES, sub),
        ("groups", "z", "core", "sub"),
    )
    tokens = P(("groups", "z", "core", "sub"), None)
    table = P(("z", "core"), None, "sub")
    return jax.shard_map(
        local,
        mesh=inner,
        in_specs=(tokens, tokens, tokens, table, table),
        out_specs=tokens,
        check_vma=False,
    )
```

```python
import functools
import math

import jax
import jax.numpy as jnp
from jax import lax
from jax.experimental import pallas as pl
from jax.experimental.pallas import tpu as pltpu
from jax.sharding import Mesh, PartitionSpec as P

CORES = 2
TERMS = 3
NT = (((1,), (1,)), ((), ()))
TN = (((0,), (0,)), ((), ()))


def pack_kernel(experts, extra, latent_ref, routes_ref, gates_ref, out_ref):
    block, width = latent_ref.shape
    out_ref[:block, :] = latent_ref[...]
    ids = lax.broadcasted_iota(jnp.int32, (extra, block), 0)
    weight = jnp.zeros((extra, block), jnp.float32)
    for k in range(routes_ref.shape[0]):
        weight = weight + jnp.where(routes_ref[k : k + 1, :] == ids, gates_ref[k : k + 1, :], 0.0)
    out_ref[block:, :] = jnp.zeros((extra, width), jnp.bfloat16)
    for t in range(TERMS):
        term = weight.astype(jnp.bfloat16)
        out_ref[block:, t * block : (t + 1) * block] = term
        weight = weight - term.astype(jnp.float32)


def pack(latent, routes, gates, experts):
    block, width = latent.shape
    extra = -(-experts // 16) * 16
    return pl.pallas_call(
        functools.partial(pack_kernel, experts, extra),
        out_shape=jax.ShapeDtypeStruct((block + extra, width), jnp.bfloat16),
        in_specs=[pl.BlockSpec(memory_space=pltpu.VMEM)] * 3,
        out_specs=pl.BlockSpec(memory_space=pltpu.VMEM),
        compiler_params=pltpu.CompilerParams(vmem_limit_bytes=4 * 1024 * 1024),
    )(latent, routes.T, gates.T)


def stage_kernel(after_ref, *refs):
    number = (len(refs) - 1) // 2
    copies = [
        pltpu.make_async_copy(refs[n], refs[number + n], refs[-1].at[n]) for n in range(number)
    ]
    for copy in copies:
        copy.start()
    for copy in copies:
        copy.wait()


def stage(after, arrays):
    return pl.pallas_call(
        stage_kernel,
        out_shape=[jax.ShapeDtypeStruct(a.shape, a.dtype) for a in arrays],
        in_specs=[pl.BlockSpec(memory_space=pl.ANY)]
        + [pl.BlockSpec(memory_space=pltpu.HBM)] * len(arrays),
        out_specs=[pl.BlockSpec(memory_space=pltpu.VMEM)] * len(arrays),
        scratch_shapes=[pltpu.SemaphoreType.DMA((len(arrays),))],
        compiler_params=pltpu.CompilerParams(vmem_limit_bytes=16 * 1024 * 1024),
    )(after, *arrays)


def expert_kernel(block, slots, unit, number, blocks, waits, *refs):
    first, core = lax.axis_index("z") * number, lax.axis_index("core")
    refs = refs[waits:]
    x_refs, tables, out_refs = refs[:blocks], refs[blocks : blocks + 2 * number], refs[blocks + 2 * number :]
    extra = x_refs[0].shape[0] - block
    earlier = lax.broadcasted_iota(jnp.int32, (block, block), 0)
    later = lax.broadcasted_iota(jnp.int32, (block, block), 1)
    before = (earlier < later).astype(jnp.bfloat16)
    groups = [range(g, min(g + unit, blocks)) for g in range(0, blocks, unit)]
    sizes = [-(-len(g) * slots // 16) * 16 for g in groups]
    row = lax.broadcasted_iota(jnp.int32, (extra, block), 0)
    gates, ranks = [], []
    for x_ref in x_refs:
        gate = 0.0
        for t in range(TERMS):
            gate = gate + x_ref[block:, t * block : (t + 1) * block].astype(jnp.float32)
        gates.append(gate)
        ranks.append(
            jnp.dot((gate > 0).astype(jnp.bfloat16), before, preferred_element_type=jnp.float32)
        )
    sums = [0.0] * blocks
    for n in range(number):
        up_ref, down_ref = tables[2 * n], tables[2 * n + 1]
        mine = row == first + lax.rem(core + number - n, number)
        picks, scales, rows = [], [], []
        for group, size in zip(groups, sizes):
            slot = lax.broadcasted_iota(jnp.int32, (size, block), 0)
            parts = []
            scale = 0.0
            for j, b in enumerate(group):
                weight = jnp.sum(jnp.where(mine, gates[b], 0.0), axis=0, keepdims=True)
                rank = jnp.sum(jnp.where(mine, ranks[b], 0.0), axis=0, keepdims=True)
                here = (slot == rank.astype(jnp.int32) + j * slots) & (weight > 0)
                scale = scale + jnp.sum(jnp.where(here, weight, 0.0), axis=1, keepdims=True)
                parts.append(here.astype(jnp.bfloat16))
            tokens = [x_refs[b][:block, :] for b in group]
            pick = jnp.concatenate(parts, axis=1) if len(group) > 1 else parts[0]
            token = jnp.concatenate(tokens, axis=0) if len(group) > 1 else tokens[0]
            rows.append(
                jnp.dot(pick, token, preferred_element_type=jnp.float32).astype(jnp.bfloat16)
            )
            picks.append(parts)
            scales.append(scale)
        picked = jnp.concatenate(rows, axis=0) if len(rows) > 1 else rows[0]
        preact = lax.dot_general(picked, up_ref[0], NT, preferred_element_type=jnp.float32)
        active = jnp.square(jnp.maximum(preact, 0.0)).astype(jnp.bfloat16)
        summed = jnp.dot(active, down_ref[0], preferred_element_type=jnp.float32)
        start = 0
        for g, (group, size) in enumerate(zip(groups, sizes)):
            gated = (summed[start : start + size] * scales[g]).astype(jnp.bfloat16)
            start += size
            for j, b in enumerate(group):
                sums[b] = sums[b] + lax.dot_general(
                    picks[g][j], gated, TN, preferred_element_type=jnp.float32
                )
    for b in range(blocks):
        out_refs[b][...] = sums[b].astype(out_refs[b].dtype)


def run_experts(after, arrived, tables, kinds, block, slots):
    blocks, number = len(arrived), len(tables) // 2
    hidden, width = tables[0].shape[1:]
    unit = 16 // math.gcd(16, slots)
    whole = pl.BlockSpec(memory_space=pltpu.VMEM)
    return pl.pallas_call(
        functools.partial(expert_kernel, block, slots, unit, number, blocks, len(after)),
        out_shape=[jax.ShapeDtypeStruct((block, width), kind) for kind in kinds],
        in_specs=[pl.BlockSpec(memory_space=pl.ANY)] * len(after)
        + [whole] * (blocks + len(tables)),
        out_specs=[whole] * blocks,
        compiler_params=pltpu.CompilerParams(vmem_limit_bytes=30 * 1024 * 1024),
        cost_estimate=pl.CostEstimate(
            flops=4 * number * blocks * slots * width * (hidden + block),
            bytes_accessed=5 * blocks * block * width + 2 * len(tables) * width * hidden,
            transcendentals=0,
        ),
    )(*after, *arrived, *tables)


def shift(array, axis, step):
    size = lax.axis_size(axis)
    return lax.ppermute(array, axis, [(i, (i + step) % size) for i in range(size)])


def follow(array, first):
    return lax.optimization_barrier((array, first))[0]


def local(latent, routes, gates, up_weight, down_weight):
    block, width = latent.shape
    top = routes.shape[1]
    cores, depth, subs = (lax.axis_size(a) for a in ("core", "z", "sub"))
    experts = depth * cores
    slots = min(block, 3 * block * top // (2 * experts))
    own = [jnp.swapaxes(up_weight, 1, 2), jnp.swapaxes(down_weight, 1, 2)]
    moved = [shift(table, "core", step) for step in range(1, cores) for table in own]
    ring = [pack(latent, routes, gates, experts)]
    tables = [*stage(ring[0], own), *moved]
    ring.append(follow(shift(ring[0], "z", 1), tables[0]))
    last = depth - 1
    kept, others = {}, {}
    totals, home = {}, None
    firsts = []

    def total(r, *behind):
        rows = kept[r]
        for s, other in enumerate(others[r], 1):
            other = shift(other, "sub", -s)
            for first in behind:
                other = follow(other, first)
            rows = rows + other.astype(jnp.float32)
        return rows

    for j in range(depth):
        handed = [shift(ring[j], "sub", s) for s in range(1, subs)]
        fresh = ([0] if j == 0 else []) + [j + 1] * (j < last)
        kinds = [jnp.bfloat16] * len(handed)
        kinds += [jnp.bfloat16 if r == 1 else jnp.float32 for r in fresh]
        after = firsts[-1:]
        if j == last and j > 1:
            rows = follow(shift(kept[1], "z", -1), firsts[-1])
            home = kept[0] + rows.astype(jnp.float32)
            after = after + [home]
        if j > 3:
            totals[j - 2] = total(j - 2, firsts[-1]).astype(jnp.bfloat16)
            after = after + [totals[j - 2]]
        partial = run_experts(after, handed + [ring[r] for r in fresh], tables, kinds, block, slots)
        firsts.append(partial[0])
        if j + 2 < depth:
            ring.append(follow(shift(ring[-1], "z", 1), partial[0]))
        for r, rows in zip(fresh, partial[subs - 1 :]):
            kept[r] = rows
        others[j] = partial[: subs - 1]
    if home is None:
        home = kept[0] + sum(shift(kept[r], "z", -r).astype(jnp.float32) for r in range(1, depth))
    joined = others[0]
    if depth > 1:
        joined = [
            (
                mine.astype(jnp.float32)
                + shift(follow(rows, ring[last]), "z", -1).astype(jnp.float32)
            ).astype(jnp.bfloat16)
            for mine, rows in zip(others[0], others[1])
        ]
    for r in range(2, depth):
        if r not in totals:
            behind = [firsts[-1]] + (joined if r < last else [totals[r - 1]] * (r > 2))
            totals[r] = total(r, *behind).astype(jnp.bfloat16)
    came = []
    for r in range(2, depth):
        rows = shift(totals[r], "z", -r)
        came.append(follow(rows, came[-1]) if came else rows)
    for s, rows in enumerate(joined, 1):
        if came:
            rows = follow(shift(follow(rows, totals[last]), "sub", -s), came[-1])
        else:
            rows = shift(rows, "sub", -s)
        home = home + rows.astype(jnp.float32)
    for rows in came:
        home = home + rows.astype(jnp.float32)
    return home.astype(jnp.bfloat16)


def solution(mesh):
    groups, experts, sub = (mesh.shape[a] for a in ("groups", "expert", "sub"))
    inner = Mesh(
        mesh.devices.reshape(groups, experts // CORES, CORES, sub),
        ("groups", "z", "core", "sub"),
    )
    tokens = P(("groups", "z", "core", "sub"), None)
    table = P(("z", "core"), None, "sub")
    return jax.shard_map(
        local,
        mesh=inner,
        in_specs=(tokens, tokens, tokens, table, table),
        out_specs=tokens,
        check_vma=False,
    )
```

```python
import functools
import math

import jax
import jax.numpy as jnp
from jax import lax
from jax.experimental import pallas as pl
from jax.experimental.pallas import tpu as pltpu
from jax.sharding import Mesh, PartitionSpec as P

CORES = 2
TERMS = 3
NT = (((1,), (1,)), ((), ()))
TN = (((0,), (0,)), ((), ()))


def pack_kernel(experts, extra, latent_ref, routes_ref, gates_ref, out_ref):
    block, width = latent_ref.shape
    out_ref[:block, :] = latent_ref[...]
    ids = lax.broadcasted_iota(jnp.int32, (extra, block), 0)
    weight = jnp.zeros((extra, block), jnp.float32)
    for k in range(routes_ref.shape[0]):
        weight = weight + jnp.where(routes_ref[k : k + 1, :] == ids, gates_ref[k : k + 1, :], 0.0)
    out_ref[block:, :] = jnp.zeros((extra, width), jnp.bfloat16)
    for t in range(TERMS):
        term = weight.astype(jnp.bfloat16)
        out_ref[block:, t * block : (t + 1) * block] = term
        weight = weight - term.astype(jnp.float32)


def pack(latent, routes, gates, experts):
    block, width = latent.shape
    extra = -(-experts // 16) * 16
    return pl.pallas_call(
        functools.partial(pack_kernel, experts, extra),
        out_shape=jax.ShapeDtypeStruct((block + extra, width), jnp.bfloat16),
        in_specs=[pl.BlockSpec(memory_space=pltpu.VMEM)] * 3,
        out_specs=pl.BlockSpec(memory_space=pltpu.VMEM),
        compiler_params=pltpu.CompilerParams(vmem_limit_bytes=4 * 1024 * 1024),
    )(latent, routes.T, gates.T)


def stage_kernel(after_ref, *refs):
    number = (len(refs) - 1) // 2
    copies = [
        pltpu.make_async_copy(refs[n], refs[number + n], refs[-1].at[n]) for n in range(number)
    ]
    for copy in copies:
        copy.start()
    for copy in copies:
        copy.wait()


def stage(after, arrays):
    return pl.pallas_call(
        stage_kernel,
        out_shape=[jax.ShapeDtypeStruct(a.shape, a.dtype) for a in arrays],
        in_specs=[pl.BlockSpec(memory_space=pl.ANY)]
        + [pl.BlockSpec(memory_space=pltpu.HBM)] * len(arrays),
        out_specs=[pl.BlockSpec(memory_space=pltpu.VMEM)] * len(arrays),
        scratch_shapes=[pltpu.SemaphoreType.DMA((len(arrays),))],
        compiler_params=pltpu.CompilerParams(vmem_limit_bytes=16 * 1024 * 1024),
    )(after, *arrays)


def expert_kernel(block, slots, unit, number, blocks, waits, *refs):
    first, core = lax.axis_index("z") * number, lax.axis_index("core")
    refs = refs[waits:]
    x_refs, tables, out_refs = refs[:blocks], refs[blocks : blocks + 2 * number], refs[blocks + 2 * number :]
    extra = x_refs[0].shape[0] - block
    earlier = lax.broadcasted_iota(jnp.int32, (block, block), 0)
    later = lax.broadcasted_iota(jnp.int32, (block, block), 1)
    before = (earlier < later).astype(jnp.bfloat16)
    groups = [range(g, min(g + unit, blocks)) for g in range(0, blocks, unit)]
    sizes = [-(-len(g) * slots // 16) * 16 for g in groups]
    row = lax.broadcasted_iota(jnp.int32, (extra, block), 0)
    gates, ranks = [], []
    for x_ref in x_refs:
        gate = 0.0
        for t in range(TERMS):
            gate = gate + x_ref[block:, t * block : (t + 1) * block].astype(jnp.float32)
        gates.append(gate)
        ranks.append(
            jnp.dot((gate > 0).astype(jnp.bfloat16), before, preferred_element_type=jnp.float32)
        )
    sums = [0.0] * blocks
    for n in range(number):
        up_ref, down_ref = tables[2 * n], tables[2 * n + 1]
        mine = row == first + lax.rem(core + number - n, number)
        picks, scales, rows = [], [], []
        for group, size in zip(groups, sizes):
            slot = lax.broadcasted_iota(jnp.int32, (size, block), 0)
            parts = []
            scale = 0.0
            for j, b in enumerate(group):
                weight = jnp.sum(jnp.where(mine, gates[b], 0.0), axis=0, keepdims=True)
                rank = jnp.sum(jnp.where(mine, ranks[b], 0.0), axis=0, keepdims=True)
                here = (slot == rank.astype(jnp.int32) + j * slots) & (weight > 0)
                scale = scale + jnp.sum(jnp.where(here, weight, 0.0), axis=1, keepdims=True)
                parts.append(here.astype(jnp.bfloat16))
            tokens = [x_refs[b][:block, :] for b in group]
            pick = jnp.concatenate(parts, axis=1) if len(group) > 1 else parts[0]
            token = jnp.concatenate(tokens, axis=0) if len(group) > 1 else tokens[0]
            rows.append(
                jnp.dot(pick, token, preferred_element_type=jnp.float32).astype(jnp.bfloat16)
            )
            picks.append(parts)
            scales.append(scale)
        picked = jnp.concatenate(rows, axis=0) if len(rows) > 1 else rows[0]
        preact = lax.dot_general(picked, up_ref[0], NT, preferred_element_type=jnp.float32)
        active = jnp.square(jnp.maximum(preact, 0.0)).astype(jnp.bfloat16)
        summed = jnp.dot(active, down_ref[0], preferred_element_type=jnp.float32)
        start = 0
        for g, (group, size) in enumerate(zip(groups, sizes)):
            gated = (summed[start : start + size] * scales[g]).astype(jnp.bfloat16)
            start += size
            for j, b in enumerate(group):
                sums[b] = sums[b] + lax.dot_general(
                    picks[g][j], gated, TN, preferred_element_type=jnp.float32
                )
    b = 0
    for out_ref in out_refs:
        for start in range(0, out_ref.shape[0], block):
            out_ref[start : start + block, :] = sums[b].astype(out_ref.dtype)
            b += 1


def run_experts(after, arrived, tables, kinds, block, slots):
    blocks, number = len(arrived), len(tables) // 2
    hidden, width = tables[0].shape[1:]
    unit = 16 // math.gcd(16, slots)
    whole = pl.BlockSpec(memory_space=pltpu.VMEM)
    return pl.pallas_call(
        functools.partial(expert_kernel, block, slots, unit, number, blocks, len(after)),
        out_shape=[jax.ShapeDtypeStruct((count * block, width), kind) for kind, count in kinds],
        in_specs=[pl.BlockSpec(memory_space=pl.ANY)] * len(after)
        + [whole] * (blocks + len(tables)),
        out_specs=[whole] * len(kinds),
        compiler_params=pltpu.CompilerParams(vmem_limit_bytes=30 * 1024 * 1024),
        cost_estimate=pl.CostEstimate(
            flops=4 * number * blocks * slots * width * (hidden + block),
            bytes_accessed=5 * blocks * block * width + 2 * len(tables) * width * hidden,
            transcendentals=0,
        ),
    )(*after, *arrived, *tables)


def shift(array, axis, step):
    size = lax.axis_size(axis)
    return lax.ppermute(array, axis, [(i, (i + step) % size) for i in range(size)])


def follow(array, first):
    return lax.optimization_barrier((array, first))[0]


def local(latent, routes, gates, up_weight, down_weight):
    block, width = latent.shape
    top = routes.shape[1]
    cores, depth, subs = (lax.axis_size(a) for a in ("core", "z", "sub"))
    experts = depth * cores
    slots = min(block, 3 * block * top // (2 * experts))
    own = [jnp.swapaxes(up_weight, 1, 2), jnp.swapaxes(down_weight, 1, 2)]
    moved = [shift(table, "core", step) for step in range(1, cores) for table in own]
    ring = [pack(latent, routes, gates, experts)]
    tables = [*stage(ring[0], own), *moved]
    ring.append(follow(shift(ring[0], "z", 1), tables[0]))
    last = depth - 1
    kept, others = {}, {}
    totals = {}
    firsts = []

    def total(r, *behind):
        rows = kept[r]
        for s, other in enumerate(others[r], 1):
            other = shift(other, "sub", -s)
            for first in behind:
                other = follow(other, first)
            rows = rows + other.astype(jnp.float32)
        return rows

    for j in range(depth):
        handed = [shift(ring[j], "sub", s) for s in range(1, subs)]
        fresh = [[0], [1, 2][:last]][j] if j < 2 else [j + 1][: last - j]
        kinds = [(jnp.bfloat16, 1)] * len(handed) + [(jnp.float32, 1)] * len(fresh)
        if j == 1:
            kinds = [(jnp.bfloat16, subs)] + kinds[subs:]
        after = firsts[-1:]
        if j > 3:
            totals[j - 2] = total(j - 2, firsts[-1]).astype(jnp.bfloat16)
            after = after + [totals[j - 2]]
        partial = run_experts(after, handed + [ring[r] for r in fresh], tables, kinds, block, slots)
        firsts.append(partial[0])
        if j + 2 < depth:
            ring.append(follow(shift(ring[-1], "z", 1), partial[0]))
        if j == 1:
            joint, *partial = partial
            fresh = fresh[1:]
        else:
            others[j], partial = partial[: subs - 1], partial[subs - 1 :]
        for r, rows in zip(fresh, partial):
            kept[r] = rows
    home, joined = kept[0], others[0]
    if depth > 1:
        sent = follow(shift(follow(joint, ring[last]), "z", -1), firsts[-1])
        sent = [sent[s * block : (s + 1) * block].astype(jnp.float32) for s in range(subs)]
        joined = [
            (mine.astype(jnp.float32) + rows).astype(jnp.bfloat16)
            for mine, rows in zip(others[0], sent)
        ]
        home = home + sent[-1]
    for r in range(2, depth):
        if r not in totals:
            behind = [firsts[-1]] + ([home, *joined] if r < last else [totals[r - 1]] * (r > 2))
            totals[r] = total(r, *behind).astype(jnp.bfloat16)
    came = []
    for r in range(2, depth):
        rows = shift(totals[r], "z", -r)
        came.append(follow(rows, came[-1]) if came else rows)
    for s, rows in enumerate(joined, 1):
        if came:
            rows = follow(shift(follow(rows, totals[last]), "sub", -s), came[-1])
        else:
            rows = shift(rows, "sub", -s)
        home = home + rows.astype(jnp.float32)
    for rows in came:
        home = home + rows.astype(jnp.float32)
    return home.astype(jnp.bfloat16)


def solution(mesh):
    groups, experts, sub = (mesh.shape[a] for a in ("groups", "expert", "sub"))
    inner = Mesh(
        mesh.devices.reshape(groups, experts // CORES, CORES, sub),
        ("groups", "z", "core", "sub"),
    )
    tokens = P(("groups", "z", "core", "sub"), None)
    table = P(("z", "core"), None, "sub")
    return jax.shard_map(
        local,
        mesh=inner,
        in_specs=(tokens, tokens, tokens, table, table),
        out_specs=tokens,
        check_vma=False,
    )
```

```python
import functools
import math

import jax
import jax.numpy as jnp
from jax import lax
from jax.experimental import pallas as pl
from jax.experimental.pallas import tpu as pltpu
from jax.sharding import Mesh, PartitionSpec as P

CORES = 2
NT = (((1,), (1,)), ((), ()))
TN = (((0,), (0,)), ((), ()))


def stage_kernel(*refs):
    number = (len(refs) - 1) // 2
    copies = [
        pltpu.make_async_copy(refs[n], refs[number + n], refs[-1].at[n]) for n in range(number)
    ]
    for copy in copies:
        copy.start()
    for copy in copies:
        copy.wait()


def stage(arrays):
    return pl.pallas_call(
        stage_kernel,
        out_shape=[jax.ShapeDtypeStruct(a.shape, a.dtype) for a in arrays],
        in_specs=[pl.BlockSpec(memory_space=pltpu.HBM)] * len(arrays),
        out_specs=[pl.BlockSpec(memory_space=pltpu.VMEM)] * len(arrays),
        scratch_shapes=[pltpu.SemaphoreType.DMA((len(arrays),))],
        compiler_params=pltpu.CompilerParams(vmem_limit_bytes=16 * 1024 * 1024),
    )(*arrays)


def expert_kernel(block, slots, unit, number, sources, waits, gates_ref, *refs):
    core, z, sub = (lax.axis_index(a) for a in ("core", "z", "sub"))
    depth, subs = lax.axis_size("z"), lax.axis_size("sub")
    blocks = len(sources)
    refs = refs[waits:]
    x_refs, tables, out_refs = refs[:blocks], refs[blocks : blocks + 2 * number], refs[blocks + 2 * number :]
    earlier = lax.broadcasted_iota(jnp.int32, (block, block), 0)
    later = lax.broadcasted_iota(jnp.int32, (block, block), 1)
    before = (earlier < later).astype(jnp.bfloat16)
    groups = [range(g, min(g + unit, blocks)) for g in range(0, blocks, unit)]
    sizes = [-(-len(g) * slots // 16) * 16 for g in groups]
    row = lax.broadcasted_iota(jnp.int32, (number, block), 0)
    gates, ranks = [], []
    for r, turn in sources:
        source = lax.rem(z + depth - r, depth) * subs + lax.rem(sub + subs - turn, subs)
        gate = gates_ref[source]
        gates.append(gate)
        ranks.append(
            jnp.dot((gate > 0).astype(jnp.bfloat16), before, preferred_element_type=jnp.float32)
        )
    sums = [0.0] * blocks
    for n in range(number):
        up_ref, down_ref = tables[2 * n], tables[2 * n + 1]
        mine = row == lax.rem(core + number - n, number)
        picks, scales, rows = [], [], []
        for group, size in zip(groups, sizes):
            slot = lax.broadcasted_iota(jnp.int32, (size, block), 0)
            parts = []
            scale = 0.0
            for j, b in enumerate(group):
                weight = jnp.sum(jnp.where(mine, gates[b], 0.0), axis=0, keepdims=True)
                rank = jnp.sum(jnp.where(mine, ranks[b], 0.0), axis=0, keepdims=True)
                here = (slot == rank.astype(jnp.int32) + j * slots) & (weight > 0)
                scale = scale + jnp.sum(jnp.where(here, weight, 0.0), axis=1, keepdims=True)
                parts.append(here.astype(jnp.bfloat16))
            tokens = [x_refs[b][...] for b in group]
            pick = jnp.concatenate(parts, axis=1) if len(group) > 1 else parts[0]
            token = jnp.concatenate(tokens, axis=0) if len(group) > 1 else tokens[0]
            rows.append(
                jnp.dot(pick, token, preferred_element_type=jnp.float32).astype(jnp.bfloat16)
            )
            picks.append(parts)
            scales.append(scale)
        picked = jnp.concatenate(rows, axis=0) if len(rows) > 1 else rows[0]
        preact = lax.dot_general(picked, up_ref[0], NT, preferred_element_type=jnp.float32)
        active = jnp.square(jnp.maximum(preact, 0.0)).astype(jnp.bfloat16)
        summed = jnp.dot(active, down_ref[0], preferred_element_type=jnp.float32)
        start = 0
        for g, (group, size) in enumerate(zip(groups, sizes)):
            gated = (summed[start : start + size] * scales[g]).astype(jnp.bfloat16)
            start += size
            for j, b in enumerate(group):
                sums[b] = sums[b] + lax.dot_general(
                    picks[g][j], gated, TN, preferred_element_type=jnp.float32
                )
    for b in range(blocks):
        out_refs[b][...] = sums[b].astype(out_refs[b].dtype)


def run_experts(after, gates, sources, arrived, tables, kinds, slots):
    blocks, number, block = len(arrived), gates.shape[1], gates.shape[2]
    hidden, width = tables[0].shape[1:]
    unit = 16 // math.gcd(16, slots)
    whole = pl.BlockSpec(memory_space=pltpu.VMEM)
    return pl.pallas_call(
        functools.partial(expert_kernel, block, slots, unit, number, sources, len(after)),
        out_shape=[jax.ShapeDtypeStruct((block, width), kind) for kind in kinds],
        in_specs=[whole]
        + [pl.BlockSpec(memory_space=pl.ANY)] * len(after)
        + [whole] * (blocks + len(tables)),
        out_specs=[whole] * blocks,
        compiler_params=pltpu.CompilerParams(vmem_limit_bytes=30 * 1024 * 1024),
        cost_estimate=pl.CostEstimate(
            flops=4 * number * blocks * slots * width * (hidden + block),
            bytes_accessed=5 * blocks * block * width + 2 * len(tables) * width * hidden,
            transcendentals=0,
        ),
    )(gates, *after, *arrived, *tables)


def shift(array, axis, step):
    size = lax.axis_size(axis)
    return lax.ppermute(array, axis, [(i, (i + step) % size) for i in range(size)])


def follow(array, first):
    return lax.optimization_barrier((array, first))[0]


def local(latent, routes, gates, up_weight, down_weight):
    block, width = latent.shape
    top = routes.shape[1]
    cores, depth, subs = (lax.axis_size(a) for a in ("core", "z", "sub"))
    experts = depth * cores
    slots = min(block, 3 * block * top // (2 * experts))
    own = [jnp.swapaxes(up_weight, 1, 2), jnp.swapaxes(down_weight, 1, 2)]
    moved = [shift(table, "core", step) for step in range(1, cores) for table in own]
    ring = [latent]
    tables = [*stage(own), *moved]
    ring.append(follow(shift(ring[0], "z", 1), tables[0]))
    ids = jnp.arange(experts, dtype=jnp.int32)
    weight = jnp.sum(
        jnp.where(routes.T[None] == ids[:, None, None], gates.T[None], 0.0), axis=1
    ).reshape(depth, 1, cores, block)
    weight = jnp.broadcast_to(weight, (depth, subs, cores, block)).reshape(-1, cores, block)
    weight = lax.all_to_all(weight, ("z", "sub"), split_axis=0, concat_axis=0, tiled=True)
    last = depth - 1
    kept, others = {}, {}
    totals, home = {}, None
    firsts = []

    def total(r, *behind):
        rows = kept[r]
        for s, other in enumerate(others[r], 1):
            other = shift(other, "sub", -s)
            for first in behind:
                other = follow(other, first)
            rows = rows + other.astype(jnp.float32)
        return rows

    for j in range(depth):
        handed = [shift(ring[j], "sub", s) for s in range(1, subs)]
        fresh = ([0] if j == 0 else []) + [j + 1] * (j < last)
        kinds = [jnp.bfloat16] * len(handed)
        kinds += [jnp.bfloat16 if r == 1 else jnp.float32 for r in fresh]
        after = firsts[-1:]
        if j == last and j > 1:
            rows = follow(shift(kept[1], "z", -1), firsts[-1])
            home = kept[0] + rows.astype(jnp.float32)
            after = after + [home]
        if j > 3:
            totals[j - 2] = total(j - 2, firsts[-1]).astype(jnp.bfloat16)
            after = after + [totals[j - 2]]
        sources = [(j, s) for s in range(1, subs)] + [(r, 0) for r in fresh]
        arrived = handed + [ring[r] for r in fresh]
        partial = run_experts(after, weight, sources, arrived, tables, kinds, slots)
        firsts.append(partial[0])
        if j + 2 < depth:
            ring.append(follow(shift(ring[-1], "z", 1), partial[0]))
        for r, rows in zip(fresh, partial[subs - 1 :]):
            kept[r] = rows
        others[j] = partial[: subs - 1]
    if home is None:
        home = kept[0] + sum(shift(kept[r], "z", -r).astype(jnp.float32) for r in range(1, depth))
    joined = others[0]
    if depth > 1:
        joined = [
            (
                mine.astype(jnp.float32)
                + shift(follow(rows, ring[last]), "z", -1).astype(jnp.float32)
            ).astype(jnp.bfloat16)
            for mine, rows in zip(others[0], others[1])
        ]
    for r in range(2, depth):
        if r not in totals:
            behind = [firsts[-1]] + (joined if r < last else [totals[r - 1]] * (r > 2))
            totals[r] = total(r, *behind).astype(jnp.bfloat16)
    came = []
    for r in range(2, depth):
        rows = shift(totals[r], "z", -r)
        came.append(follow(rows, came[-1]) if came else rows)
    for s, rows in enumerate(joined, 1):
        if came:
            rows = follow(shift(follow(rows, totals[last]), "sub", -s), came[-1])
        else:
            rows = shift(rows, "sub", -s)
        home = home + rows.astype(jnp.float32)
    for rows in came:
        home = home + rows.astype(jnp.float32)
    return home.astype(jnp.bfloat16)


def solution(mesh):
    groups, experts, sub = (mesh.shape[a] for a in ("groups", "expert", "sub"))
    inner = Mesh(
        mesh.devices.reshape(groups, experts // CORES, CORES, sub),
        ("groups", "z", "core", "sub"),
    )
    tokens = P(("groups", "z", "core", "sub"), None)
    table = P(("z", "core"), None, "sub")
    return jax.shard_map(
        local,
        mesh=inner,
        in_specs=(tokens, tokens, tokens, table, table),
        out_specs=tokens,
        check_vma=False,
    )
```

```python
import functools
import math

import jax
import jax.numpy as jnp
from jax import lax
from jax.experimental import pallas as pl
from jax.experimental.pallas import tpu as pltpu
from jax.sharding import Mesh, PartitionSpec as P

CORES = 2
NT = (((1,), (1,)), ((), ()))
TN = (((0,), (0,)), ((), ()))


def stage_kernel(*refs):
    number = (len(refs) - 1) // 2
    copies = [
        pltpu.make_async_copy(refs[n], refs[number + n], refs[-1].at[n]) for n in range(number)
    ]
    for copy in copies:
        copy.start()
    for copy in copies:
        copy.wait()


def stage(arrays):
    return pl.pallas_call(
        stage_kernel,
        out_shape=[jax.ShapeDtypeStruct(a.shape, a.dtype) for a in arrays],
        in_specs=[pl.BlockSpec(memory_space=pltpu.HBM)] * len(arrays),
        out_specs=[pl.BlockSpec(memory_space=pltpu.VMEM)] * len(arrays),
        scratch_shapes=[pltpu.SemaphoreType.DMA((len(arrays),))],
        compiler_params=pltpu.CompilerParams(vmem_limit_bytes=16 * 1024 * 1024),
    )(*arrays)


def expert_kernel(block, slots, unit, number, sources, waits, *refs):
    rounds = sorted({r for r, _ in sources})
    gate_refs, refs = refs[: len(rounds)], refs[len(rounds) :]
    first, core = lax.axis_index("z") * number, lax.axis_index("core")
    blocks, experts = len(sources), gate_refs[0].shape[0] // lax.axis_size("sub")
    refs = refs[waits:]
    x_refs, tables, out_refs = refs[:blocks], refs[blocks : blocks + 2 * number], refs[blocks + 2 * number :]
    earlier = lax.broadcasted_iota(jnp.int32, (block, block), 0)
    later = lax.broadcasted_iota(jnp.int32, (block, block), 1)
    before = (earlier < later).astype(jnp.bfloat16)
    groups = [range(g, min(g + unit, blocks)) for g in range(0, blocks, unit)]
    sizes = [-(-len(g) * slots // 16) * 16 for g in groups]
    row = lax.broadcasted_iota(jnp.int32, (experts, block), 0)
    gates, ranks = [], []
    for r, turn in sources:
        gate = gate_refs[rounds.index(r)][turn * experts : (turn + 1) * experts, :]
        gates.append(gate)
        ranks.append(
            jnp.dot((gate > 0).astype(jnp.bfloat16), before, preferred_element_type=jnp.float32)
        )
    sums = [0.0] * blocks
    for n in range(number):
        up_ref, down_ref = tables[2 * n], tables[2 * n + 1]
        mine = row == first + lax.rem(core + number - n, number)
        picks, scales, rows = [], [], []
        for group, size in zip(groups, sizes):
            slot = lax.broadcasted_iota(jnp.int32, (size, block), 0)
            parts = []
            scale = 0.0
            for j, b in enumerate(group):
                weight = jnp.sum(jnp.where(mine, gates[b], 0.0), axis=0, keepdims=True)
                rank = jnp.sum(jnp.where(mine, ranks[b], 0.0), axis=0, keepdims=True)
                here = (slot == rank.astype(jnp.int32) + j * slots) & (weight > 0)
                scale = scale + jnp.sum(jnp.where(here, weight, 0.0), axis=1, keepdims=True)
                parts.append(here.astype(jnp.bfloat16))
            tokens = [x_refs[b][...] for b in group]
            pick = jnp.concatenate(parts, axis=1) if len(group) > 1 else parts[0]
            token = jnp.concatenate(tokens, axis=0) if len(group) > 1 else tokens[0]
            rows.append(
                jnp.dot(pick, token, preferred_element_type=jnp.float32).astype(jnp.bfloat16)
            )
            picks.append(parts)
            scales.append(scale)
        picked = jnp.concatenate(rows, axis=0) if len(rows) > 1 else rows[0]
        preact = lax.dot_general(picked, up_ref[0], NT, preferred_element_type=jnp.float32)
        active = jnp.square(jnp.maximum(preact, 0.0)).astype(jnp.bfloat16)
        summed = jnp.dot(active, down_ref[0], preferred_element_type=jnp.float32)
        start = 0
        for g, (group, size) in enumerate(zip(groups, sizes)):
            gated = (summed[start : start + size] * scales[g]).astype(jnp.bfloat16)
            start += size
            for j, b in enumerate(group):
                sums[b] = sums[b] + lax.dot_general(
                    picks[g][j], gated, TN, preferred_element_type=jnp.float32
                )
    for b in range(blocks):
        out_refs[b][...] = sums[b].astype(out_refs[b].dtype)


def run_experts(after, gates, sources, arrived, tables, kinds, slots):
    blocks, number, block = len(arrived), len(tables) // 2, gates[0].shape[1]
    gates = [gates[r] for r in sorted({r for r, _ in sources})]
    hidden, width = tables[0].shape[1:]
    unit = 16 // math.gcd(16, slots)
    whole = pl.BlockSpec(memory_space=pltpu.VMEM)
    return pl.pallas_call(
        functools.partial(expert_kernel, block, slots, unit, number, sources, len(after)),
        out_shape=[jax.ShapeDtypeStruct((block, width), kind) for kind in kinds],
        in_specs=[whole] * len(gates)
        + [pl.BlockSpec(memory_space=pl.ANY)] * len(after)
        + [whole] * (blocks + len(tables)),
        out_specs=[whole] * blocks,
        compiler_params=pltpu.CompilerParams(vmem_limit_bytes=30 * 1024 * 1024),
        cost_estimate=pl.CostEstimate(
            flops=4 * number * blocks * slots * width * (hidden + block),
            bytes_accessed=5 * blocks * block * width + 2 * len(tables) * width * hidden,
            transcendentals=0,
        ),
    )(*gates, *after, *arrived, *tables)


def shift(array, axis, step):
    size = lax.axis_size(axis)
    return lax.ppermute(array, axis, [(i, (i + step) % size) for i in range(size)])


def follow(array, first):
    return lax.optimization_barrier((array, first))[0]


def local(latent, routes, gates, up_weight, down_weight):
    block, width = latent.shape
    top = routes.shape[1]
    cores, depth, subs = (lax.axis_size(a) for a in ("core", "z", "sub"))
    experts = depth * cores
    slots = min(block, 3 * block * top // (2 * experts))
    own = [jnp.swapaxes(up_weight, 1, 2), jnp.swapaxes(down_weight, 1, 2)]
    moved = [shift(table, "core", step) for step in range(1, cores) for table in own]
    ring = [latent]
    tables = [*stage(own), *moved]
    ring.append(follow(shift(ring[0], "z", 1), tables[0]))
    ids = jnp.arange(experts, dtype=jnp.int32)
    weight = jnp.sum(
        jnp.where(routes.T[None] == ids[:, None, None], gates.T[None], 0.0), axis=1
    )
    near = [weight] + [follow(shift(weight, "sub", s), tables[0]) for s in range(1, subs)]
    near = jnp.concatenate(near, axis=0)
    weights = [near] + [shift(near, "z", r) for r in range(1, depth)]
    last = depth - 1
    kept, others = {}, {}
    totals, home = {}, None
    firsts = []

    def total(r, *behind):
        rows = kept[r]
        for s, other in enumerate(others[r], 1):
            other = shift(other, "sub", -s)
            for first in behind:
                other = follow(other, first)
            rows = rows + other.astype(jnp.float32)
        return rows

    for j in range(depth):
        handed = [shift(ring[j], "sub", s) for s in range(1, subs)]
        fresh = ([0] if j == 0 else []) + [j + 1] * (j < last)
        kinds = [jnp.bfloat16] * len(handed)
        kinds += [jnp.bfloat16 if r == 1 else jnp.float32 for r in fresh]
        after = firsts[-1:]
        if j == last and j > 1:
            rows = follow(shift(kept[1], "z", -1), firsts[-1])
            home = kept[0] + rows.astype(jnp.float32)
            after = after + [home]
        if j > 3:
            totals[j - 2] = total(j - 2, firsts[-1]).astype(jnp.bfloat16)
            after = after + [totals[j - 2]]
        sources = [(j, s) for s in range(1, subs)] + [(r, 0) for r in fresh]
        arrived = handed + [ring[r] for r in fresh]
        partial = run_experts(after, weights, sources, arrived, tables, kinds, slots)
        firsts.append(partial[0])
        if j + 2 < depth:
            ring.append(follow(shift(ring[-1], "z", 1), partial[0]))
        for r, rows in zip(fresh, partial[subs - 1 :]):
            kept[r] = rows
        others[j] = partial[: subs - 1]
    if home is None:
        home = kept[0] + sum(shift(kept[r], "z", -r).astype(jnp.float32) for r in range(1, depth))
    joined = others[0]
    if depth > 1:
        joined = [
            (
                mine.astype(jnp.float32)
                + shift(follow(rows, ring[last]), "z", -1).astype(jnp.float32)
            ).astype(jnp.bfloat16)
            for mine, rows in zip(others[0], others[1])
        ]
    for r in range(2, depth):
        if r not in totals:
            behind = [firsts[-1]] + (joined if r < last else [totals[r - 1]] * (r > 2))
            totals[r] = total(r, *behind).astype(jnp.bfloat16)
    came = []
    for r in range(2, depth):
        rows = shift(totals[r], "z", -r)
        came.append(follow(rows, came[-1]) if came else rows)
    for s, rows in enumerate(joined, 1):
        if came:
            rows = follow(shift(follow(rows, totals[last]), "sub", -s), came[-1])
        else:
            rows = shift(rows, "sub", -s)
        home = home + rows.astype(jnp.float32)
    for rows in came:
        home = home + rows.astype(jnp.float32)
    return home.astype(jnp.bfloat16)


def solution(mesh):
    groups, experts, sub = (mesh.shape[a] for a in ("groups", "expert", "sub"))
    inner = Mesh(
        mesh.devices.reshape(groups, experts // CORES, CORES, sub),
        ("groups", "z", "core", "sub"),
    )
    tokens = P(("groups", "z", "core", "sub"), None)
    table = P(("z", "core"), None, "sub")
    return jax.shard_map(
        local,
        mesh=inner,
        in_specs=(tokens, tokens, tokens, table, table),
        out_specs=tokens,
        check_vma=False,
    )
```

```python
import functools
import math

import jax
import jax.numpy as jnp
from jax import lax
from jax.experimental import pallas as pl
from jax.experimental.pallas import tpu as pltpu
from jax.sharding import Mesh, PartitionSpec as P

CORES = 2
NT = (((1,), (1,)), ((), ()))
TN = (((0,), (0,)), ((), ()))


def stage_kernel(*refs):
    number = (len(refs) - 1) // 2
    copies = [
        pltpu.make_async_copy(refs[n], refs[number + n], refs[-1].at[n]) for n in range(number)
    ]
    for copy in copies:
        copy.start()
    for copy in copies:
        copy.wait()


def stage(arrays):
    return pl.pallas_call(
        stage_kernel,
        out_shape=[jax.ShapeDtypeStruct(a.shape, a.dtype) for a in arrays],
        in_specs=[pl.BlockSpec(memory_space=pltpu.HBM)] * len(arrays),
        out_specs=[pl.BlockSpec(memory_space=pltpu.VMEM)] * len(arrays),
        scratch_shapes=[pltpu.SemaphoreType.DMA((len(arrays),))],
        compiler_params=pltpu.CompilerParams(vmem_limit_bytes=16 * 1024 * 1024),
    )(*arrays)


def expert_kernel(block, slots, unit, number, sources, waits, *refs):
    rounds = sorted({r for r, _ in sources})
    gate_refs, refs = refs[: len(rounds)], refs[len(rounds) :]
    first, core = lax.axis_index("z") * number, lax.axis_index("core")
    blocks, experts = len(sources), gate_refs[0].shape[0] // lax.axis_size("sub")
    refs = refs[waits:]
    x_refs, tables, out_refs = refs[:blocks], refs[blocks : blocks + 2 * number], refs[blocks + 2 * number :]
    earlier = lax.broadcasted_iota(jnp.int32, (block, block), 0)
    later = lax.broadcasted_iota(jnp.int32, (block, block), 1)
    before = (earlier < later).astype(jnp.bfloat16)
    groups = [range(g, min(g + unit, blocks)) for g in range(0, blocks, unit)]
    sizes = [-(-len(g) * slots // 16) * 16 for g in groups]
    row = lax.broadcasted_iota(jnp.int32, (experts, block), 0)
    gates, ranks = [], []
    for r, turn in sources:
        gate = gate_refs[rounds.index(r)][turn * experts : (turn + 1) * experts, :]
        gates.append(gate)
        ranks.append(
            jnp.dot((gate > 0).astype(jnp.bfloat16), before, preferred_element_type=jnp.float32)
        )
    sums = [0.0] * blocks
    for n in range(number):
        up_ref, down_ref = tables[2 * n], tables[2 * n + 1]
        mine = row == first + lax.rem(core + number - n, number)
        picks, scales, rows = [], [], []
        for group, size in zip(groups, sizes):
            slot = lax.broadcasted_iota(jnp.int32, (size, block), 0)
            parts = []
            scale = 0.0
            for j, b in enumerate(group):
                weight = jnp.sum(jnp.where(mine, gates[b], 0.0), axis=0, keepdims=True)
                rank = jnp.sum(jnp.where(mine, ranks[b], 0.0), axis=0, keepdims=True)
                here = (slot == rank.astype(jnp.int32) + j * slots) & (weight > 0)
                scale = scale + jnp.sum(jnp.where(here, weight, 0.0), axis=1, keepdims=True)
                parts.append(here.astype(jnp.bfloat16))
            tokens = [x_refs[b][...] for b in group]
            pick = jnp.concatenate(parts, axis=1) if len(group) > 1 else parts[0]
            token = jnp.concatenate(tokens, axis=0) if len(group) > 1 else tokens[0]
            rows.append(
                jnp.dot(pick, token, preferred_element_type=jnp.float32).astype(jnp.bfloat16)
            )
            picks.append(parts)
            scales.append(scale)
        picked = jnp.concatenate(rows, axis=0) if len(rows) > 1 else rows[0]
        preact = lax.dot_general(picked, up_ref[0], NT, preferred_element_type=jnp.float32)
        active = jnp.square(jnp.maximum(preact, 0.0)).astype(jnp.bfloat16)
        summed = jnp.dot(active, down_ref[0], preferred_element_type=jnp.float32)
        start = 0
        for g, (group, size) in enumerate(zip(groups, sizes)):
            gated = (summed[start : start + size] * scales[g]).astype(jnp.bfloat16)
            start += size
            for j, b in enumerate(group):
                sums[b] = sums[b] + lax.dot_general(
                    picks[g][j], gated, TN, preferred_element_type=jnp.float32
                )
    for b in range(blocks):
        out_refs[b][...] = sums[b].astype(out_refs[b].dtype)


def run_experts(after, gates, sources, arrived, tables, kinds, slots):
    blocks, number, block = len(arrived), len(tables) // 2, gates[0].shape[1]
    gates = [gates[r] for r in sorted({r for r, _ in sources})]
    hidden, width = tables[0].shape[1:]
    unit = 16 // math.gcd(16, slots)
    whole = pl.BlockSpec(memory_space=pltpu.VMEM)
    return pl.pallas_call(
        functools.partial(expert_kernel, block, slots, unit, number, sources, len(after)),
        out_shape=[jax.ShapeDtypeStruct((block, width), kind) for kind in kinds],
        in_specs=[whole] * len(gates)
        + [pl.BlockSpec(memory_space=pl.ANY)] * len(after)
        + [whole] * (blocks + len(tables)),
        out_specs=[whole] * blocks,
        compiler_params=pltpu.CompilerParams(vmem_limit_bytes=30 * 1024 * 1024),
        cost_estimate=pl.CostEstimate(
            flops=4 * number * blocks * slots * width * (hidden + block),
            bytes_accessed=5 * blocks * block * width + 2 * len(tables) * width * hidden,
            transcendentals=0,
        ),
    )(*gates, *after, *arrived, *tables)


def shift(array, axis, step):
    size = lax.axis_size(axis)
    return lax.ppermute(array, axis, [(i, (i + step) % size) for i in range(size)])


def follow(array, first):
    return lax.optimization_barrier((array, first))[0]


def local(latent, routes, gates, up_weight, down_weight):
    block, width = latent.shape
    top = routes.shape[1]
    cores, depth, subs = (lax.axis_size(a) for a in ("core", "z", "sub"))
    experts = depth * cores
    slots = min(block, 3 * block * top // (2 * experts))
    own = [jnp.swapaxes(up_weight, 1, 2), jnp.swapaxes(down_weight, 1, 2)]
    moved = [shift(table, "core", step) for step in range(1, cores) for table in own]
    ring = [latent]
    tables = [*stage(own), *moved]
    ring.append(follow(shift(ring[0], "z", 1), tables[0]))
    ids = jnp.arange(experts, dtype=jnp.int32)
    weight = jnp.sum(
        jnp.where(routes.T[None] == ids[:, None, None], gates.T[None], 0.0), axis=1
    )
    near = [weight] + [follow(shift(weight, "sub", s), tables[0]) for s in range(1, subs)]
    near = jnp.concatenate(near, axis=0)
    weights = [near] + [shift(near, "z", r) for r in range(1, depth)]
    last = depth - 1
    kept, others = {}, {}
    totals, home = {}, None
    firsts = []

    def total(r, *behind):
        rows = kept[r]
        for s, other in enumerate(others[r], 1):
            other = shift(other, "sub", -s)
            for first in behind:
                other = follow(other, first)
            rows = rows + other.astype(jnp.float32)
        return rows

    for j in range(depth):
        handed = [shift(ring[j], "sub", s) for s in range(1, subs)]
        fresh = ([0] if j == 0 else []) + [j + 1] * (j < last)
        kinds = [jnp.bfloat16] * len(handed)
        kinds += [jnp.bfloat16 if r == 1 else jnp.float32 for r in fresh]
        after = firsts[-1:]
        if j == last and j > 1:
            home = kept[0] + shift(follow(kept[1], ring[last]), "z", -1).astype(jnp.float32)
        if j > 3:
            totals[j - 2] = total(j - 2, firsts[-1]).astype(jnp.bfloat16)
            after = after + [totals[j - 2]]
        sources = [(j, s) for s in range(1, subs)] + [(r, 0) for r in fresh]
        arrived = handed + [ring[r] for r in fresh]
        partial = run_experts(after, weights, sources, arrived, tables, kinds, slots)
        firsts.append(partial[0])
        if j + 2 < depth:
            ring.append(follow(shift(ring[-1], "z", 1), partial[0]))
        for r, rows in zip(fresh, partial[subs - 1 :]):
            kept[r] = rows
        others[j] = partial[: subs - 1]
    if home is None:
        home = kept[0] + sum(shift(kept[r], "z", -r).astype(jnp.float32) for r in range(1, depth))
    joined = others[0]
    if depth > 1:
        joined = [
            (
                mine.astype(jnp.float32)
                + shift(follow(rows, ring[last]), "z", -1).astype(jnp.float32)
            ).astype(jnp.bfloat16)
            for mine, rows in zip(others[0], others[1])
        ]
    for r in range(2, depth):
        if r not in totals:
            behind = [firsts[-1]] + ([home, *joined] if r < last else [totals[r - 1]] * (r > 2))
            totals[r] = total(r, *behind).astype(jnp.bfloat16)
    came = []
    for r in range(2, depth):
        rows = shift(totals[r], "z", -r)
        came.append(follow(rows, came[-1]) if came else rows)
    for s, rows in enumerate(joined, 1):
        if came:
            rows = follow(shift(follow(rows, totals[last]), "sub", -s), came[-1])
        else:
            rows = shift(rows, "sub", -s)
        home = home + rows.astype(jnp.float32)
    for rows in came:
        home = home + rows.astype(jnp.float32)
    return home.astype(jnp.bfloat16)


def solution(mesh):
    groups, experts, sub = (mesh.shape[a] for a in ("groups", "expert", "sub"))
    inner = Mesh(
        mesh.devices.reshape(groups, experts // CORES, CORES, sub),
        ("groups", "z", "core", "sub"),
    )
    tokens = P(("groups", "z", "core", "sub"), None)
    table = P(("z", "core"), None, "sub")
    return jax.shard_map(
        local,
        mesh=inner,
        in_specs=(tokens, tokens, tokens, table, table),
        out_specs=tokens,
        check_vma=False,
    )
```

```python
import functools
import math

import jax
import jax.numpy as jnp
from jax import lax
from jax.experimental import pallas as pl
from jax.experimental.pallas import tpu as pltpu
from jax.sharding import Mesh, PartitionSpec as P

CORES = 2
NT = (((1,), (1,)), ((), ()))
TN = (((0,), (0,)), ((), ()))


def stage_kernel(*refs):
    number = (len(refs) - 1) // 2
    copies = [
        pltpu.make_async_copy(refs[n], refs[number + n], refs[-1].at[n]) for n in range(number)
    ]
    for copy in copies:
        copy.start()
    for copy in copies:
        copy.wait()


def stage(arrays):
    return pl.pallas_call(
        stage_kernel,
        out_shape=[jax.ShapeDtypeStruct(a.shape, a.dtype) for a in arrays],
        in_specs=[pl.BlockSpec(memory_space=pltpu.HBM)] * len(arrays),
        out_specs=[pl.BlockSpec(memory_space=pltpu.VMEM)] * len(arrays),
        scratch_shapes=[pltpu.SemaphoreType.DMA((len(arrays),))],
        compiler_params=pltpu.CompilerParams(vmem_limit_bytes=16 * 1024 * 1024),
    )(*arrays)


def expert_kernel(block, slots, unit, number, sources, waits, *refs):
    rounds = sorted({r for r, _ in sources})
    gate_refs, refs = refs[: len(rounds)], refs[len(rounds) :]
    first, core = lax.axis_index("z") * number, lax.axis_index("core")
    blocks, experts = len(sources), gate_refs[0].shape[0] // lax.axis_size("sub")
    refs = refs[waits:]
    x_refs, tables, out_refs = refs[:blocks], refs[blocks : blocks + 2 * number], refs[blocks + 2 * number :]
    earlier = lax.broadcasted_iota(jnp.int32, (block, block), 0)
    later = lax.broadcasted_iota(jnp.int32, (block, block), 1)
    before = (earlier < later).astype(jnp.bfloat16)
    groups = [range(g, min(g + unit, blocks)) for g in range(0, blocks, unit)]
    sizes = [-(-len(g) * slots // 16) * 16 for g in groups]
    row = lax.broadcasted_iota(jnp.int32, (experts, block), 0)
    gates, ranks = [], []
    for r, turn in sources:
        gate = gate_refs[rounds.index(r)][turn * experts : (turn + 1) * experts, :]
        gates.append(gate)
        ranks.append(
            jnp.dot((gate > 0).astype(jnp.bfloat16), before, preferred_element_type=jnp.float32)
        )
    sums = [0.0] * blocks
    for n in range(number):
        up_ref, down_ref = tables[2 * n], tables[2 * n + 1]
        mine = row == first + lax.rem(core + number - n, number)
        picks, scales, rows = [], [], []
        for group, size in zip(groups, sizes):
            slot = lax.broadcasted_iota(jnp.int32, (size, block), 0)
            parts = []
            scale = 0.0
            for j, b in enumerate(group):
                weight = jnp.sum(jnp.where(mine, gates[b], 0.0), axis=0, keepdims=True)
                rank = jnp.sum(jnp.where(mine, ranks[b], 0.0), axis=0, keepdims=True)
                here = (slot == rank.astype(jnp.int32) + j * slots) & (weight > 0)
                scale = scale + jnp.sum(jnp.where(here, weight, 0.0), axis=1, keepdims=True)
                parts.append(here.astype(jnp.bfloat16))
            tokens = [x_refs[b][...] for b in group]
            pick = jnp.concatenate(parts, axis=1) if len(group) > 1 else parts[0]
            token = jnp.concatenate(tokens, axis=0) if len(group) > 1 else tokens[0]
            rows.append(
                jnp.dot(pick, token, preferred_element_type=jnp.float32).astype(jnp.bfloat16)
            )
            picks.append(parts)
            scales.append(scale)
        picked = jnp.concatenate(rows, axis=0) if len(rows) > 1 else rows[0]
        preact = lax.dot_general(picked, up_ref[0], NT, preferred_element_type=jnp.float32)
        active = jnp.square(jnp.maximum(preact, 0.0)).astype(jnp.bfloat16)
        summed = jnp.dot(active, down_ref[0], preferred_element_type=jnp.float32)
        start = 0
        for g, (group, size) in enumerate(zip(groups, sizes)):
            gated = (summed[start : start + size] * scales[g]).astype(jnp.bfloat16)
            start += size
            for j, b in enumerate(group):
                sums[b] = sums[b] + lax.dot_general(
                    picks[g][j], gated, TN, preferred_element_type=jnp.float32
                )
    for b in range(blocks):
        out_refs[b][...] = sums[b].astype(out_refs[b].dtype)


def run_experts(after, gates, sources, arrived, tables, kinds, slots):
    blocks, number, block = len(arrived), len(tables) // 2, gates[0].shape[1]
    gates = [gates[r] for r in sorted({r for r, _ in sources})]
    hidden, width = tables[0].shape[1:]
    unit = 16 // math.gcd(16, slots)
    whole = pl.BlockSpec(memory_space=pltpu.VMEM)
    return pl.pallas_call(
        functools.partial(expert_kernel, block, slots, unit, number, sources, len(after)),
        out_shape=[jax.ShapeDtypeStruct((block, width), kind) for kind in kinds],
        in_specs=[whole] * len(gates)
        + [pl.BlockSpec(memory_space=pl.ANY)] * len(after)
        + [whole] * (blocks + len(tables)),
        out_specs=[whole] * blocks,
        compiler_params=pltpu.CompilerParams(vmem_limit_bytes=30 * 1024 * 1024),
        cost_estimate=pl.CostEstimate(
            flops=4 * number * blocks * slots * width * (hidden + block),
            bytes_accessed=5 * blocks * block * width + 2 * len(tables) * width * hidden,
            transcendentals=0,
        ),
    )(*gates, *after, *arrived, *tables)


def shift(array, axis, step):
    size = lax.axis_size(axis)
    return lax.ppermute(array, axis, [(i, (i + step) % size) for i in range(size)])


def follow(array, first):
    return lax.optimization_barrier((array, first))[0]


def local(latent, routes, gates, up_weight, down_weight):
    block, width = latent.shape
    top = routes.shape[1]
    cores, depth, subs = (lax.axis_size(a) for a in ("core", "z", "sub"))
    experts = depth * cores
    slots = min(block, 3 * block * top // (2 * experts))
    own = [jnp.swapaxes(up_weight, 1, 2), jnp.swapaxes(down_weight, 1, 2)]
    moved = [shift(table, "core", step) for step in range(1, cores) for table in own]
    ring = [latent]
    tables = [*stage(own), *moved]
    ring.append(follow(shift(ring[0], "z", 1), tables[0]))
    ids = jnp.arange(experts, dtype=jnp.int32)
    weight = jnp.sum(
        jnp.where(routes.T[None] == ids[:, None, None], gates.T[None], 0.0), axis=1
    )
    near = [weight] + [follow(shift(weight, "sub", s), tables[0]) for s in range(1, subs)]
    near = jnp.concatenate(near, axis=0)
    weights = [near] + [shift(near, "z", r) for r in range(1, depth)]
    last = depth - 1
    kept, others = {}, {}
    totals, home = {}, None
    firsts = []

    def total(r, *behind):
        rows = kept[r]
        for s, other in enumerate(others[r], 1):
            other = shift(other, "sub", -s)
            for first in behind:
                other = follow(other, first)
            rows = rows + other.astype(jnp.float32)
        return rows

    for j in range(depth):
        handed = [shift(ring[j], "sub", s) for s in range(1, subs)]
        fresh = ([0] if j == 0 else []) + [j + 1] * (j < last)
        kinds = [jnp.bfloat16] * len(handed)
        kinds += [jnp.bfloat16 if r == 1 else jnp.float32 for r in fresh]
        after = firsts[-1:] + (weights[3:] if j == 1 else [])
        if j == last and j > 1:
            home = kept[0] + shift(follow(kept[1], firsts[-1]), "z", -1).astype(jnp.float32)
        if j > 3:
            totals[j - 2] = total(j - 2, firsts[-1]).astype(jnp.bfloat16)
            after = after + [totals[j - 2]]
        sources = [(j, s) for s in range(1, subs)] + [(r, 0) for r in fresh]
        arrived = handed + [ring[r] for r in fresh]
        partial = run_experts(after, weights, sources, arrived, tables, kinds, slots)
        firsts.append(partial[0])
        if j + 2 < depth:
            ring.append(follow(shift(ring[-1], "z", 1), partial[0]))
        for r, rows in zip(fresh, partial[subs - 1 :]):
            kept[r] = rows
        others[j] = partial[: subs - 1]
    if home is None:
        home = kept[0] + sum(shift(kept[r], "z", -r).astype(jnp.float32) for r in range(1, depth))
    joined = others[0]
    if depth > 1:
        joined = [
            (
                mine.astype(jnp.float32)
                + shift(follow(rows, firsts[max(last - 1, 1)]), "z", -1).astype(jnp.float32)
            ).astype(jnp.bfloat16)
            for mine, rows in zip(others[0], others[1])
        ]
    for r in range(2, depth):
        if r not in totals:
            behind = [firsts[-1]] + ([home, *joined] if r < last else [totals[r - 1]] * (r > 2))
            totals[r] = total(r, *behind).astype(jnp.bfloat16)
    came = []
    for r in range(2, depth):
        rows = shift(totals[r], "z", -r)
        came.append(follow(rows, came[-1]) if came else rows)
    for s, rows in enumerate(joined, 1):
        if came:
            rows = follow(shift(follow(rows, totals[last]), "sub", -s), came[-1])
        else:
            rows = shift(rows, "sub", -s)
        home = home + rows.astype(jnp.float32)
    for rows in came:
        home = home + rows.astype(jnp.float32)
    return home.astype(jnp.bfloat16)


def solution(mesh):
    groups, experts, sub = (mesh.shape[a] for a in ("groups", "expert", "sub"))
    inner = Mesh(
        mesh.devices.reshape(groups, experts // CORES, CORES, sub),
        ("groups", "z", "core", "sub"),
    )
    tokens = P(("groups", "z", "core", "sub"), None)
    table = P(("z", "core"), None, "sub")
    return jax.shard_map(
        local,
        mesh=inner,
        in_specs=(tokens, tokens, tokens, table, table),
        out_specs=tokens,
        check_vma=False,
    )
```

```python
import functools
import math

import jax
import jax.numpy as jnp
from jax import lax
from jax.experimental import pallas as pl
from jax.experimental.pallas import tpu as pltpu
from jax.sharding import Mesh, PartitionSpec as P

CORES = 2
NT = (((1,), (1,)), ((), ()))
TN = (((0,), (0,)), ((), ()))


def stage_kernel(*refs):
    number = (len(refs) - 1) // 2
    copies = [
        pltpu.make_async_copy(refs[n], refs[number + n], refs[-1].at[n]) for n in range(number)
    ]
    for copy in copies:
        copy.start()
    for copy in copies:
        copy.wait()


def stage(arrays):
    return pl.pallas_call(
        stage_kernel,
        out_shape=[jax.ShapeDtypeStruct(a.shape, a.dtype) for a in arrays],
        in_specs=[pl.BlockSpec(memory_space=pltpu.HBM)] * len(arrays),
        out_specs=[pl.BlockSpec(memory_space=pltpu.VMEM)] * len(arrays),
        scratch_shapes=[pltpu.SemaphoreType.DMA((len(arrays),))],
        compiler_params=pltpu.CompilerParams(vmem_limit_bytes=16 * 1024 * 1024),
    )(*arrays)


def expert_kernel(block, slots, unit, number, sources, waits, *refs):
    steps = sorted({r.bit_length() for r, _ in sources})
    gate_refs, refs = refs[: len(steps)], refs[len(steps) :]
    first, core = lax.axis_index("z") * number, lax.axis_index("core")
    blocks, experts, subs = len(sources), lax.axis_size("z") * number, lax.axis_size("sub")
    refs = refs[waits:]
    x_refs, tables, out_refs = refs[:blocks], refs[blocks : blocks + 2 * number], refs[blocks + 2 * number :]
    earlier = lax.broadcasted_iota(jnp.int32, (block, block), 0)
    later = lax.broadcasted_iota(jnp.int32, (block, block), 1)
    before = (earlier < later).astype(jnp.bfloat16)
    groups = [range(g, min(g + unit, blocks)) for g in range(0, blocks, unit)]
    sizes = [-(-len(g) * slots // 16) * 16 for g in groups]
    row = lax.broadcasted_iota(jnp.int32, (experts, block), 0)
    gates, ranks = [], []
    for r, turn in sources:
        place = ((r - (2 ** r.bit_length()) // 2 * (r > 0)) * subs + turn) * experts
        gate = gate_refs[steps.index(r.bit_length())][place : place + experts, :]
        gates.append(gate)
        ranks.append(
            jnp.dot((gate > 0).astype(jnp.bfloat16), before, preferred_element_type=jnp.float32)
        )
    sums = [0.0] * blocks
    for n in range(number):
        up_ref, down_ref = tables[2 * n], tables[2 * n + 1]
        mine = row == first + lax.rem(core + number - n, number)
        picks, scales, rows = [], [], []
        for group, size in zip(groups, sizes):
            slot = lax.broadcasted_iota(jnp.int32, (size, block), 0)
            parts = []
            scale = 0.0
            for j, b in enumerate(group):
                weight = jnp.sum(jnp.where(mine, gates[b], 0.0), axis=0, keepdims=True)
                rank = jnp.sum(jnp.where(mine, ranks[b], 0.0), axis=0, keepdims=True)
                here = (slot == rank.astype(jnp.int32) + j * slots) & (weight > 0)
                scale = scale + jnp.sum(jnp.where(here, weight, 0.0), axis=1, keepdims=True)
                parts.append(here.astype(jnp.bfloat16))
            tokens = [x_refs[b][...] for b in group]
            pick = jnp.concatenate(parts, axis=1) if len(group) > 1 else parts[0]
            token = jnp.concatenate(tokens, axis=0) if len(group) > 1 else tokens[0]
            rows.append(
                jnp.dot(pick, token, preferred_element_type=jnp.float32).astype(jnp.bfloat16)
            )
            picks.append(parts)
            scales.append(scale)
        picked = jnp.concatenate(rows, axis=0) if len(rows) > 1 else rows[0]
        preact = lax.dot_general(picked, up_ref[0], NT, preferred_element_type=jnp.float32)
        active = jnp.square(jnp.maximum(preact, 0.0)).astype(jnp.bfloat16)
        summed = jnp.dot(active, down_ref[0], preferred_element_type=jnp.float32)
        start = 0
        for g, (group, size) in enumerate(zip(groups, sizes)):
            gated = (summed[start : start + size] * scales[g]).astype(jnp.bfloat16)
            start += size
            for j, b in enumerate(group):
                sums[b] = sums[b] + lax.dot_general(
                    picks[g][j], gated, TN, preferred_element_type=jnp.float32
                )
    for b in range(blocks):
        out_refs[b][...] = sums[b].astype(out_refs[b].dtype)


def run_experts(after, gates, sources, arrived, tables, kinds, slots):
    blocks, number, block = len(arrived), len(tables) // 2, gates[0].shape[1]
    gates = [gates[step] for step in sorted({r.bit_length() for r, _ in sources})]
    hidden, width = tables[0].shape[1:]
    unit = 16 // math.gcd(16, slots)
    whole = pl.BlockSpec(memory_space=pltpu.VMEM)
    return pl.pallas_call(
        functools.partial(expert_kernel, block, slots, unit, number, sources, len(after)),
        out_shape=[jax.ShapeDtypeStruct((block, width), kind) for kind in kinds],
        in_specs=[whole] * len(gates)
        + [pl.BlockSpec(memory_space=pl.ANY)] * len(after)
        + [whole] * (blocks + len(tables)),
        out_specs=[whole] * blocks,
        compiler_params=pltpu.CompilerParams(vmem_limit_bytes=30 * 1024 * 1024),
        cost_estimate=pl.CostEstimate(
            flops=4 * number * blocks * slots * width * (hidden + block),
            bytes_accessed=5 * blocks * block * width + 2 * len(tables) * width * hidden,
            transcendentals=0,
        ),
    )(*gates, *after, *arrived, *tables)


def shift(array, axis, step):
    size = lax.axis_size(axis)
    return lax.ppermute(array, axis, [(i, (i + step) % size) for i in range(size)])


def follow(array, first):
    return lax.optimization_barrier((array, first))[0]


def local(latent, routes, gates, up_weight, down_weight):
    block, width = latent.shape
    top = routes.shape[1]
    cores, depth, subs = (lax.axis_size(a) for a in ("core", "z", "sub"))
    experts = depth * cores
    slots = min(block, 3 * block * top // (2 * experts))
    own = [jnp.swapaxes(up_weight, 1, 2), jnp.swapaxes(down_weight, 1, 2)]
    moved = [shift(table, "core", step) for step in range(1, cores) for table in own]
    ring = [latent]
    tables = [*stage(own), *moved]
    ring.append(follow(shift(ring[0], "z", 1), tables[0]))
    ids = jnp.arange(experts, dtype=jnp.int32)
    weight = jnp.sum(
        jnp.where(routes.T[None] == ids[:, None, None], gates.T[None], 0.0), axis=1
    )
    near = [weight] + [follow(shift(weight, "sub", s), tables[0]) for s in range(1, subs)]
    near = jnp.concatenate(near, axis=0)
    weights, held = [near], near
    while 2 ** len(weights) < 2 * depth:
        weights.append(shift(held, "z", 2 ** (len(weights) - 1)))
        held = jnp.concatenate([held, weights[-1]], axis=0)
    last = depth - 1
    kept, others = {}, {}
    totals, home = {}, None
    firsts = []

    def total(r, *behind):
        rows = kept[r]
        for s, other in enumerate(others[r], 1):
            other = shift(other, "sub", -s)
            for first in behind:
                other = follow(other, first)
            rows = rows + other.astype(jnp.float32)
        return rows

    for j in range(depth):
        handed = [shift(ring[j], "sub", s) for s in range(1, subs)]
        fresh = ([0] if j == 0 else []) + [j + 1] * (j < last)
        kinds = [jnp.bfloat16] * len(handed)
        kinds += [jnp.bfloat16 if r == 1 else jnp.float32 for r in fresh]
        after = firsts[-1:]
        if j == last and j > 1:
            home = kept[0] + shift(follow(kept[1], ring[last]), "z", -1).astype(jnp.float32)
        if j > 3:
            totals[j - 2] = total(j - 2, firsts[-1]).astype(jnp.bfloat16)
            after = after + [totals[j - 2]]
        sources = [(j, s) for s in range(1, subs)] + [(r, 0) for r in fresh]
        arrived = handed + [ring[r] for r in fresh]
        partial = run_experts(after, weights, sources, arrived, tables, kinds, slots)
        firsts.append(partial[0])
        if j + 2 < depth:
            ring.append(follow(shift(ring[-1], "z", 1), partial[0]))
        for r, rows in zip(fresh, partial[subs - 1 :]):
            kept[r] = rows
        others[j] = partial[: subs - 1]
    if home is None:
        home = kept[0] + sum(shift(kept[r], "z", -r).astype(jnp.float32) for r in range(1, depth))
    joined = others[0]
    if depth > 1:
        joined = [
            (
                mine.astype(jnp.float32)
                + shift(follow(rows, ring[last]), "z", -1).astype(jnp.float32)
            ).astype(jnp.bfloat16)
            for mine, rows in zip(others[0], others[1])
        ]
    for r in range(2, depth):
        if r not in totals:
            behind = [firsts[-1]] + ([home, *joined] if r < last else [totals[r - 1]] * (r > 2))
            totals[r] = total(r, *behind).astype(jnp.bfloat16)
    came = []
    for r in range(2, depth):
        rows = shift(totals[r], "z", -r)
        came.append(follow(rows, came[-1]) if came else rows)
    for s, rows in enumerate(joined, 1):
        if came:
            rows = follow(shift(follow(rows, totals[last]), "sub", -s), came[-1])
        else:
            rows = shift(rows, "sub", -s)
        home = home + rows.astype(jnp.float32)
    for rows in came:
        home = home + rows.astype(jnp.float32)
    return home.astype(jnp.bfloat16)


def solution(mesh):
    groups, experts, sub = (mesh.shape[a] for a in ("groups", "expert", "sub"))
    inner = Mesh(
        mesh.devices.reshape(groups, experts // CORES, CORES, sub),
        ("groups", "z", "core", "sub"),
    )
    tokens = P(("groups", "z", "core", "sub"), None)
    table = P(("z", "core"), None, "sub")
    return jax.shard_map(
        local,
        mesh=inner,
        in_specs=(tokens, tokens, tokens, table, table),
        out_specs=tokens,
        check_vma=False,
    )
```

```python
import functools
import math

import jax
import jax.numpy as jnp
from jax import lax
from jax.experimental import pallas as pl
from jax.experimental.pallas import tpu as pltpu
from jax.sharding import Mesh, PartitionSpec as P

CORES = 2
NT = (((1,), (1,)), ((), ()))
TN = (((0,), (0,)), ((), ()))


def stage_kernel(*refs):
    number = (len(refs) - 1) // 2
    copies = [
        pltpu.make_async_copy(refs[n], refs[number + n], refs[-1].at[n]) for n in range(number)
    ]
    for copy in copies:
        copy.start()
    for copy in copies:
        copy.wait()


def stage(arrays):
    return pl.pallas_call(
        stage_kernel,
        out_shape=[jax.ShapeDtypeStruct(a.shape, a.dtype) for a in arrays],
        in_specs=[pl.BlockSpec(memory_space=pltpu.HBM)] * len(arrays),
        out_specs=[pl.BlockSpec(memory_space=pltpu.VMEM)] * len(arrays),
        scratch_shapes=[pltpu.SemaphoreType.DMA((len(arrays),))],
        compiler_params=pltpu.CompilerParams(vmem_limit_bytes=16 * 1024 * 1024),
    )(*arrays)


def expert_kernel(block, slots, unit, number, sources, waits, *refs):
    steps = sorted({r.bit_length() for r, _ in sources})
    gate_refs, refs = refs[: len(steps)], refs[len(steps) :]
    first, core = lax.axis_index("z") * number, lax.axis_index("core")
    blocks, experts, subs = len(sources), lax.axis_size("z") * number, lax.axis_size("sub")
    refs = refs[waits:]
    x_refs, tables, out_refs = refs[:blocks], refs[blocks : blocks + 2 * number], refs[blocks + 2 * number :]
    earlier = lax.broadcasted_iota(jnp.int32, (block, block), 0)
    later = lax.broadcasted_iota(jnp.int32, (block, block), 1)
    before = (earlier < later).astype(jnp.bfloat16)
    groups = [range(g, min(g + unit, blocks)) for g in range(0, blocks, unit)]
    sizes = [-(-len(g) * slots // 16) * 16 for g in groups]
    row = lax.broadcasted_iota(jnp.int32, (experts, block), 0)
    gates, ranks = [], []
    for r, turn in sources:
        place = ((r - (2 ** r.bit_length()) // 2 * (r > 0)) * subs + turn) * experts
        gate = gate_refs[steps.index(r.bit_length())][place : place + experts, :]
        gates.append(gate)
        ranks.append(
            jnp.dot((gate > 0).astype(jnp.bfloat16), before, preferred_element_type=jnp.float32)
        )
    sums = [0.0] * blocks
    for n in range(number):
        up_ref, down_ref = tables[2 * n], tables[2 * n + 1]
        mine = row == first + lax.rem(core + number - n, number)
        picks, scales, rows = [], [], []
        for group, size in zip(groups, sizes):
            slot = lax.broadcasted_iota(jnp.int32, (size, block), 0)
            parts = []
            scale = 0.0
            for j, b in enumerate(group):
                weight = jnp.sum(jnp.where(mine, gates[b], 0.0), axis=0, keepdims=True)
                rank = jnp.sum(jnp.where(mine, ranks[b], 0.0), axis=0, keepdims=True)
                here = (slot == rank.astype(jnp.int32) + j * slots) & (weight > 0)
                scale = scale + jnp.sum(jnp.where(here, weight, 0.0), axis=1, keepdims=True)
                parts.append(here.astype(jnp.bfloat16))
            tokens = [x_refs[b][...] for b in group]
            pick = jnp.concatenate(parts, axis=1) if len(group) > 1 else parts[0]
            token = jnp.concatenate(tokens, axis=0) if len(group) > 1 else tokens[0]
            rows.append(
                jnp.dot(pick, token, preferred_element_type=jnp.float32).astype(jnp.bfloat16)
            )
            picks.append(parts)
            scales.append(scale)
        picked = jnp.concatenate(rows, axis=0) if len(rows) > 1 else rows[0]
        preact = lax.dot_general(picked, up_ref[0], NT, preferred_element_type=jnp.float32)
        active = jnp.square(jnp.maximum(preact, 0.0)).astype(jnp.bfloat16)
        summed = jnp.dot(active, down_ref[0], preferred_element_type=jnp.float32)
        start = 0
        for g, (group, size) in enumerate(zip(groups, sizes)):
            gated = (summed[start : start + size] * scales[g]).astype(jnp.bfloat16)
            start += size
            for j, b in enumerate(group):
                sums[b] = sums[b] + lax.dot_general(
                    picks[g][j], gated, TN, preferred_element_type=jnp.float32
                )
    b = 0
    for out_ref in out_refs:
        for start in range(0, out_ref.shape[0], block):
            out_ref[start : start + block, :] = sums[b].astype(out_ref.dtype)
            b += 1


def run_experts(after, gates, sources, arrived, tables, kinds, slots):
    blocks, number, block = len(arrived), len(tables) // 2, gates[0].shape[1]
    gates = [gates[step] for step in sorted({r.bit_length() for r, _ in sources})]
    hidden, width = tables[0].shape[1:]
    unit = 16 // math.gcd(16, slots)
    whole = pl.BlockSpec(memory_space=pltpu.VMEM)
    return pl.pallas_call(
        functools.partial(expert_kernel, block, slots, unit, number, sources, len(after)),
        out_shape=[jax.ShapeDtypeStruct((count * block, width), kind) for kind, count in kinds],
        in_specs=[whole] * len(gates)
        + [pl.BlockSpec(memory_space=pl.ANY)] * len(after)
        + [whole] * (blocks + len(tables)),
        out_specs=[whole] * len(kinds),
        compiler_params=pltpu.CompilerParams(vmem_limit_bytes=30 * 1024 * 1024),
        cost_estimate=pl.CostEstimate(
            flops=4 * number * blocks * slots * width * (hidden + block),
            bytes_accessed=5 * blocks * block * width + 2 * len(tables) * width * hidden,
            transcendentals=0,
        ),
    )(*gates, *after, *arrived, *tables)


def shift(array, axis, step):
    size = lax.axis_size(axis)
    return lax.ppermute(array, axis, [(i, (i + step) % size) for i in range(size)])


def follow(array, first):
    return lax.optimization_barrier((array, first))[0]


def local(latent, routes, gates, up_weight, down_weight):
    block, width = latent.shape
    top = routes.shape[1]
    cores, depth, subs = (lax.axis_size(a) for a in ("core", "z", "sub"))
    experts = depth * cores
    slots = min(block, 3 * block * top // (2 * experts))
    own = [jnp.swapaxes(up_weight, 1, 2), jnp.swapaxes(down_weight, 1, 2)]
    moved = [shift(table, "core", step) for step in range(1, cores) for table in own]
    ring = [latent]
    tables = [*stage(own), *moved]
    ring.append(follow(shift(ring[0], "z", 1), tables[0]))
    ids = jnp.arange(experts, dtype=jnp.int32)
    weight = jnp.sum(
        jnp.where(routes.T[None] == ids[:, None, None], gates.T[None], 0.0), axis=1
    )
    near = [weight] + [follow(shift(weight, "sub", s), tables[0]) for s in range(1, subs)]
    near = jnp.concatenate(near, axis=0)
    weights, held = [near], near
    while 2 ** len(weights) < 2 * depth:
        weights.append(shift(held, "z", 2 ** (len(weights) - 1)))
        held = jnp.concatenate([held, weights[-1]], axis=0)
    last = depth - 1
    kept, others = {}, {}
    totals = {}
    firsts = []

    def total(r, *behind):
        rows = kept[r]
        for s, other in enumerate(others[r], 1):
            other = shift(other, "sub", -s)
            for first in behind:
                other = follow(other, first)
            rows = rows + other.astype(jnp.float32)
        return rows

    for j in range(depth):
        handed = [shift(ring[j], "sub", s) for s in range(1, subs)]
        fresh = [[0], [1, 2][:last]][j] if j < 2 else [j + 1][: last - j]
        kinds = [(jnp.bfloat16, 1)] * len(handed) + [(jnp.float32, 1)] * len(fresh)
        if j == 1:
            kinds = [(jnp.bfloat16, subs)] + kinds[subs:]
        after = firsts[-1:]
        if j > 3:
            totals[j - 2] = total(j - 2, firsts[-1]).astype(jnp.bfloat16)
            after = after + [totals[j - 2]]
        sources = [(j, s) for s in range(1, subs)] + [(r, 0) for r in fresh]
        arrived = handed + [ring[r] for r in fresh]
        partial = run_experts(after, weights, sources, arrived, tables, kinds, slots)
        firsts.append(partial[0])
        if j + 2 < depth:
            ring.append(follow(shift(ring[-1], "z", 1), partial[0]))
        if j == 1:
            joint, *partial = partial
            fresh = fresh[1:]
        else:
            others[j], partial = partial[: subs - 1], partial[subs - 1 :]
        for r, rows in zip(fresh, partial):
            kept[r] = rows
    home, joined = kept[0], others[0]
    if depth > 1:
        sent = follow(shift(follow(joint, ring[last]), "z", -1), firsts[-1])
        sent = [sent[s * block : (s + 1) * block].astype(jnp.float32) for s in range(subs)]
        joined = [
            (mine.astype(jnp.float32) + rows).astype(jnp.bfloat16)
            for mine, rows in zip(others[0], sent)
        ]
        home = home + sent[-1]
    for r in range(2, depth):
        if r not in totals:
            behind = [firsts[-1]] + ([totals[r - 1]] * (r > 2) + [home, *joined] if r == last else [])
            totals[r] = total(r, *behind).astype(jnp.bfloat16)
    came = []
    for r in range(2, depth):
        rows = shift(totals[r], "z", -r)
        came.append(follow(rows, came[-1]) if came else rows)
    for s, rows in enumerate(joined, 1):
        if came:
            rows = follow(shift(follow(rows, totals[last]), "sub", -s), came[-1])
        else:
            rows = shift(rows, "sub", -s)
        home = home + rows.astype(jnp.float32)
    for rows in came:
        home = home + rows.astype(jnp.float32)
    return home.astype(jnp.bfloat16)


def solution(mesh):
    groups, experts, sub = (mesh.shape[a] for a in ("groups", "expert", "sub"))
    inner = Mesh(
        mesh.devices.reshape(groups, experts // CORES, CORES, sub),
        ("groups", "z", "core", "sub"),
    )
    tokens = P(("groups", "z", "core", "sub"), None)
    table = P(("z", "core"), None, "sub")
    return jax.shard_map(
        local,
        mesh=inner,
        in_specs=(tokens, tokens, tokens, table, table),
        out_specs=tokens,
        check_vma=False,
    )
```

```python
import functools
import math

import jax
import jax.numpy as jnp
from jax import lax
from jax.experimental import pallas as pl
from jax.experimental.pallas import tpu as pltpu
from jax.sharding import Mesh, PartitionSpec as P

CORES = 2
NT = (((1,), (1,)), ((), ()))
TN = (((0,), (0,)), ((), ()))


def stage_kernel(*refs):
    number = (len(refs) - 1) // 2
    copies = [
        pltpu.make_async_copy(refs[n], refs[number + n], refs[-1].at[n]) for n in range(number)
    ]
    for copy in copies:
        copy.start()
    for copy in copies:
        copy.wait()


def stage(arrays):
    return pl.pallas_call(
        stage_kernel,
        out_shape=[jax.ShapeDtypeStruct(a.shape, a.dtype) for a in arrays],
        in_specs=[pl.BlockSpec(memory_space=pltpu.HBM)] * len(arrays),
        out_specs=[pl.BlockSpec(memory_space=pltpu.VMEM)] * len(arrays),
        scratch_shapes=[pltpu.SemaphoreType.DMA((len(arrays),))],
        compiler_params=pltpu.CompilerParams(vmem_limit_bytes=16 * 1024 * 1024),
    )(*arrays)


def expert_kernel(block, slots, unit, number, sources, waits, *refs):
    steps = sorted({r.bit_length() for r, _ in sources})
    gate_refs, refs = refs[: len(steps)], refs[len(steps) :]
    first, core = lax.axis_index("z") * number, lax.axis_index("core")
    blocks, experts, subs = len(sources), lax.axis_size("z") * number, lax.axis_size("sub")
    refs = refs[waits:]
    x_refs, tables, out_refs = refs[:blocks], refs[blocks : blocks + 2 * number], refs[blocks + 2 * number :]
    earlier = lax.broadcasted_iota(jnp.int32, (block, block), 0)
    later = lax.broadcasted_iota(jnp.int32, (block, block), 1)
    before = (earlier < later).astype(jnp.bfloat16)
    groups = [range(g, min(g + unit, blocks)) for g in range(0, blocks, unit)]
    sizes = [-(-len(g) * slots // 16) * 16 for g in groups]
    row = lax.broadcasted_iota(jnp.int32, (experts, block), 0)
    gates, ranks = [], []
    for r, turn in sources:
        place = ((r - (2 ** r.bit_length()) // 2 * (r > 0)) * subs + turn) * experts
        gate = gate_refs[steps.index(r.bit_length())][place : place + experts, :]
        gates.append(gate)
        ranks.append(
            jnp.dot((gate > 0).astype(jnp.bfloat16), before, preferred_element_type=jnp.float32)
        )
    sums = [0.0] * blocks
    for n in range(number):
        up_ref, down_ref = tables[2 * n], tables[2 * n + 1]
        mine = row == first + lax.rem(core + number - n, number)
        picks, scales, rows = [], [], []
        for group, size in zip(groups, sizes):
            slot = lax.broadcasted_iota(jnp.int32, (size, block), 0)
            parts = []
            scale = 0.0
            for j, b in enumerate(group):
                weight = jnp.sum(jnp.where(mine, gates[b], 0.0), axis=0, keepdims=True)
                rank = jnp.sum(jnp.where(mine, ranks[b], 0.0), axis=0, keepdims=True)
                here = (slot == rank.astype(jnp.int32) + j * slots) & (weight > 0)
                scale = scale + jnp.sum(jnp.where(here, weight, 0.0), axis=1, keepdims=True)
                parts.append(here.astype(jnp.bfloat16))
            tokens = [x_refs[b][...] for b in group]
            pick = jnp.concatenate(parts, axis=1) if len(group) > 1 else parts[0]
            token = jnp.concatenate(tokens, axis=0) if len(group) > 1 else tokens[0]
            rows.append(
                jnp.dot(pick, token, preferred_element_type=jnp.float32).astype(jnp.bfloat16)
            )
            picks.append(parts)
            scales.append(scale)
        picked = jnp.concatenate(rows, axis=0) if len(rows) > 1 else rows[0]
        preact = lax.dot_general(picked, up_ref[0], NT, preferred_element_type=jnp.float32)
        active = jnp.square(jnp.maximum(preact, 0.0)).astype(jnp.bfloat16)
        summed = jnp.dot(active, down_ref[0], preferred_element_type=jnp.float32)
        start = 0
        for g, (group, size) in enumerate(zip(groups, sizes)):
            gated = (summed[start : start + size] * scales[g]).astype(jnp.bfloat16)
            start += size
            for j, b in enumerate(group):
                sums[b] = sums[b] + lax.dot_general(
                    picks[g][j], gated, TN, preferred_element_type=jnp.float32
                )
    b = 0
    for out_ref in out_refs:
        for start in range(0, out_ref.shape[0], block):
            out_ref[start : start + block, :] = sums[b].astype(out_ref.dtype)
            b += 1


def run_experts(after, gates, sources, arrived, tables, kinds, slots):
    blocks, number, block = len(arrived), len(tables) // 2, gates[0].shape[1]
    gates = [gates[step] for step in sorted({r.bit_length() for r, _ in sources})]
    hidden, width = tables[0].shape[1:]
    unit = 16 // math.gcd(16, slots)
    whole = pl.BlockSpec(memory_space=pltpu.VMEM)
    return pl.pallas_call(
        functools.partial(expert_kernel, block, slots, unit, number, sources, len(after)),
        out_shape=[jax.ShapeDtypeStruct((count * block, width), kind) for kind, count in kinds],
        in_specs=[whole] * len(gates)
        + [pl.BlockSpec(memory_space=pl.ANY)] * len(after)
        + [whole] * (blocks + len(tables)),
        out_specs=[whole] * len(kinds),
        compiler_params=pltpu.CompilerParams(vmem_limit_bytes=30 * 1024 * 1024),
        cost_estimate=pl.CostEstimate(
            flops=4 * number * blocks * slots * width * (hidden + block),
            bytes_accessed=5 * blocks * block * width + 2 * len(tables) * width * hidden,
            transcendentals=0,
        ),
    )(*gates, *after, *arrived, *tables)


def shift(array, axis, step):
    size = lax.axis_size(axis)
    return lax.ppermute(array, axis, [(i, (i + step) % size) for i in range(size)])


def follow(array, first):
    return lax.optimization_barrier((array, first))[0]


def local(latent, routes, gates, up_weight, down_weight):
    block, width = latent.shape
    top = routes.shape[1]
    cores, depth, subs = (lax.axis_size(a) for a in ("core", "z", "sub"))
    experts = depth * cores
    slots = min(block, 3 * block * top // (2 * experts))
    own = [jnp.swapaxes(up_weight, 1, 2), jnp.swapaxes(down_weight, 1, 2)]
    moved = [shift(table, "core", step) for step in range(1, cores) for table in own]
    ring = [latent]
    tables = [*stage(own), *moved]
    ring.append(follow(shift(ring[0], "z", 1), tables[0]))
    ids = jnp.arange(experts, dtype=jnp.int32)
    weight = jnp.sum(
        jnp.where(routes.T[None] == ids[:, None, None], gates.T[None], 0.0), axis=1
    )
    near = [weight] + [follow(shift(weight, "sub", s), ring[1]) for s in range(1, subs)]
    near = jnp.concatenate(near, axis=0)
    weights = [near]
    last = depth - 1
    kept, others = {}, {}
    totals = {}
    firsts = []

    def total(r, *behind):
        rows = kept[r]
        for s, other in enumerate(others[r], 1):
            other = shift(other, "sub", -s)
            for first in behind:
                other = follow(other, first)
            rows = rows + other.astype(jnp.float32)
        return rows

    for j in range(depth):
        handed = [shift(ring[j], "sub", s) for s in range(1, subs)]
        fresh = [[0], [1, 2][:last]][j] if j < 2 else [j + 1][: last - j]
        kinds = [(jnp.bfloat16, 1)] * len(handed) + [(jnp.float32, 1)] * len(fresh)
        if j == 1:
            kinds = [(jnp.bfloat16, subs)] + kinds[subs:]
        after = firsts[-1:]
        if j > 3:
            totals[j - 2] = total(j - 2, firsts[-1]).astype(jnp.bfloat16)
            after = after + [totals[j - 2]]
        sources = [(j, s) for s in range(1, subs)] + [(r, 0) for r in fresh]
        arrived = handed + [ring[r] for r in fresh]
        partial = run_experts(after, weights, sources, arrived, tables, kinds, slots)
        firsts.append(partial[0])
        if j == 0:
            held = near
            while 2 ** len(weights) < 2 * depth:
                moved = shift(held, "z", 2 ** (len(weights) - 1))
                weights.append(follow(moved, partial[0]))
                held = jnp.concatenate([held, weights[-1]], axis=0)
        if j + 2 < depth:
            ring.append(follow(shift(ring[-1], "z", 1), partial[0]))
        if j == 1:
            joint, *partial = partial
            fresh = fresh[1:]
        else:
            others[j], partial = partial[: subs - 1], partial[subs - 1 :]
        for r, rows in zip(fresh, partial):
            kept[r] = rows
    home, joined = kept[0], others[0]
    if depth > 1:
        sent = follow(shift(follow(joint, ring[last]), "z", -1), firsts[-1])
        sent = [sent[s * block : (s + 1) * block].astype(jnp.float32) for s in range(subs)]
        joined = [
            (mine.astype(jnp.float32) + rows).astype(jnp.bfloat16)
            for mine, rows in zip(others[0], sent)
        ]
        home = home + sent[-1]
    for r in range(2, depth):
        if r not in totals:
            behind = [firsts[-1]] + ([totals[r - 1]] * (r > 2) + [home, *joined] if r == last else [])
            totals[r] = total(r, *behind).astype(jnp.bfloat16)
    came = []
    for r in range(2, depth):
        rows = shift(totals[r], "z", -r)
        came.append(follow(rows, came[-1]) if came else rows)
    for s, rows in enumerate(joined, 1):
        if came:
            rows = follow(shift(follow(rows, totals[last]), "sub", -s), came[-1])
        else:
            rows = shift(rows, "sub", -s)
        home = home + rows.astype(jnp.float32)
    for rows in came:
        home = home + rows.astype(jnp.float32)
    return home.astype(jnp.bfloat16)


def solution(mesh):
    groups, experts, sub = (mesh.shape[a] for a in ("groups", "expert", "sub"))
    inner = Mesh(
        mesh.devices.reshape(groups, experts // CORES, CORES, sub),
        ("groups", "z", "core", "sub"),
    )
    tokens = P(("groups", "z", "core", "sub"), None)
    table = P(("z", "core"), None, "sub")
    return jax.shard_map(
        local,
        mesh=inner,
        in_specs=(tokens, tokens, tokens, table, table),
        out_specs=tokens,
        check_vma=False,
    )
```

```python
import functools
import math

import jax
import jax.numpy as jnp
from jax import lax
from jax.experimental import pallas as pl
from jax.experimental.pallas import tpu as pltpu
from jax.sharding import Mesh, PartitionSpec as P

CORES = 2
NT = (((1,), (1,)), ((), ()))
TN = (((0,), (0,)), ((), ()))


def stage_kernel(*refs):
    number = (len(refs) - 1) // 2
    copies = [
        pltpu.make_async_copy(refs[n], refs[number + n], refs[-1].at[n]) for n in range(number)
    ]
    for copy in copies:
        copy.start()
    for copy in copies:
        copy.wait()


def stage(arrays):
    return pl.pallas_call(
        stage_kernel,
        out_shape=[jax.ShapeDtypeStruct(a.shape, a.dtype) for a in arrays],
        in_specs=[pl.BlockSpec(memory_space=pltpu.HBM)] * len(arrays),
        out_specs=[pl.BlockSpec(memory_space=pltpu.VMEM)] * len(arrays),
        scratch_shapes=[pltpu.SemaphoreType.DMA((len(arrays),))],
        compiler_params=pltpu.CompilerParams(vmem_limit_bytes=16 * 1024 * 1024),
    )(*arrays)


def expert_kernel(block, slots, unit, number, sources, waits, *refs):
    steps = sorted({r.bit_length() for r, _ in sources})
    gate_refs, refs = refs[: len(steps)], refs[len(steps) :]
    first, core = lax.axis_index("z") * number, lax.axis_index("core")
    blocks, experts, subs = len(sources), lax.axis_size("z") * number, lax.axis_size("sub")
    refs = refs[waits:]
    x_refs, tables, out_refs = refs[:blocks], refs[blocks : blocks + 2 * number], refs[blocks + 2 * number :]
    earlier = lax.broadcasted_iota(jnp.int32, (block, block), 0)
    later = lax.broadcasted_iota(jnp.int32, (block, block), 1)
    before = (earlier < later).astype(jnp.bfloat16)
    groups = [range(g, min(g + unit, blocks)) for g in range(0, blocks, unit)]
    sizes = [-(-len(g) * slots // 16) * 16 for g in groups]
    row = lax.broadcasted_iota(jnp.int32, (experts, block), 0)
    gates, ranks = [], []
    for r, turn in sources:
        place = ((r - (2 ** r.bit_length()) // 2 * (r > 0)) * subs + turn) * experts
        gate = gate_refs[steps.index(r.bit_length())][place : place + experts, :]
        gates.append(gate)
        ranks.append(
            jnp.dot((gate > 0).astype(jnp.bfloat16), before, preferred_element_type=jnp.float32)
        )
    sums = [0.0] * blocks
    for n in range(number):
        up_ref, down_ref = tables[2 * n], tables[2 * n + 1]
        mine = row == first + lax.rem(core + number - n, number)
        picks, scales, rows = [], [], []
        for group, size in zip(groups, sizes):
            slot = lax.broadcasted_iota(jnp.int32, (size, block), 0)
            parts = []
            scale = 0.0
            for j, b in enumerate(group):
                weight = jnp.sum(jnp.where(mine, gates[b], 0.0), axis=0, keepdims=True)
                rank = jnp.sum(jnp.where(mine, ranks[b], 0.0), axis=0, keepdims=True)
                here = (slot == rank.astype(jnp.int32) + j * slots) & (weight > 0)
                scale = scale + jnp.sum(jnp.where(here, weight, 0.0), axis=1, keepdims=True)
                parts.append(here.astype(jnp.bfloat16))
            tokens = [x_refs[b][...] for b in group]
            pick = jnp.concatenate(parts, axis=1) if len(group) > 1 else parts[0]
            token = jnp.concatenate(tokens, axis=0) if len(group) > 1 else tokens[0]
            rows.append(
                jnp.dot(pick, token, preferred_element_type=jnp.float32).astype(jnp.bfloat16)
            )
            picks.append(parts)
            scales.append(scale)
        picked = jnp.concatenate(rows, axis=0) if len(rows) > 1 else rows[0]
        preact = lax.dot_general(picked, up_ref[0], NT, preferred_element_type=jnp.float32)
        active = jnp.square(jnp.maximum(preact, 0.0)).astype(jnp.bfloat16)
        summed = jnp.dot(active, down_ref[0], preferred_element_type=jnp.float32)
        start = 0
        for g, (group, size) in enumerate(zip(groups, sizes)):
            gated = (summed[start : start + size] * scales[g]).astype(jnp.bfloat16)
            start += size
            for j, b in enumerate(group):
                sums[b] = sums[b] + lax.dot_general(
                    picks[g][j], gated, TN, preferred_element_type=jnp.float32
                )
    b = 0
    for out_ref in out_refs:
        for start in range(0, out_ref.shape[0], block):
            out_ref[start : start + block, :] = sums[b].astype(out_ref.dtype)
            b += 1


def run_experts(after, gates, sources, arrived, tables, kinds, slots):
    blocks, number, block = len(arrived), len(tables) // 2, gates[0].shape[1]
    gates = [gates[step] for step in sorted({r.bit_length() for r, _ in sources})]
    hidden, width = tables[0].shape[1:]
    unit = 16 // math.gcd(16, slots)
    whole = pl.BlockSpec(memory_space=pltpu.VMEM)
    return pl.pallas_call(
        functools.partial(expert_kernel, block, slots, unit, number, sources, len(after)),
        out_shape=[jax.ShapeDtypeStruct((count * block, width), kind) for kind, count in kinds],
        in_specs=[whole] * len(gates)
        + [pl.BlockSpec(memory_space=pl.ANY)] * len(after)
        + [whole] * (blocks + len(tables)),
        out_specs=[whole] * len(kinds),
        compiler_params=pltpu.CompilerParams(vmem_limit_bytes=30 * 1024 * 1024),
        cost_estimate=pl.CostEstimate(
            flops=4 * number * blocks * slots * width * (hidden + block),
            bytes_accessed=5 * blocks * block * width + 2 * len(tables) * width * hidden,
            transcendentals=0,
        ),
    )(*gates, *after, *arrived, *tables)


def shift(array, axis, step):
    size = lax.axis_size(axis)
    return lax.ppermute(array, axis, [(i, (i + step) % size) for i in range(size)])


def follow(array, first):
    return lax.optimization_barrier((array, first))[0]


def local(latent, routes, gates, up_weight, down_weight):
    block, width = latent.shape
    top = routes.shape[1]
    cores, depth, subs = (lax.axis_size(a) for a in ("core", "z", "sub"))
    experts = depth * cores
    slots = min(block, 3 * block * top // (2 * experts))
    own = [jnp.swapaxes(up_weight, 1, 2), jnp.swapaxes(down_weight, 1, 2)]
    moved = [shift(table, "core", step) for step in range(1, cores) for table in own]
    ring = [latent]
    tables = [*stage(own), *moved]
    ring.append(follow(shift(ring[0], "z", 1), tables[0]))
    ids = jnp.arange(experts, dtype=jnp.int32)
    weight = jnp.sum(
        jnp.where(routes.T[None] == ids[:, None, None], gates.T[None], 0.0), axis=1
    )
    near = [weight] + [follow(shift(weight, "sub", s), ring[1]) for s in range(1, subs)]
    near = jnp.concatenate(near, axis=0)
    weights = [near]
    last = depth - 1
    kept, others = {}, {}
    totals = {}
    firsts = []

    def total(r, *behind):
        rows = kept[r]
        for s, other in enumerate(others[r], 1):
            other = shift(other, "sub", -s)
            for first in behind:
                other = follow(other, first)
            rows = rows + other.astype(jnp.float32)
        return rows

    for j in range(depth):
        handed = [shift(ring[j], "sub", s) for s in range(1, subs)]
        fresh = [[0], [1, 2][:last]][j] if j < 2 else [j + 1][: last - j]
        kinds = [(jnp.bfloat16, 1)] * len(handed) + [(jnp.float32, 1)] * len(fresh)
        if j == 1:
            kinds = [(jnp.bfloat16, subs)] + kinds[subs:]
        after = firsts[-1:]
        if j > 3:
            totals[j - 2] = total(j - 2, firsts[-1]).astype(jnp.bfloat16)
            after = after + [totals[j - 2]]
        if j == 1 and depth > 3:
            ring.append(follow(shift(ring[-1], "z", 1), firsts[-1]))
            after = after + [ring[-1]]
        sources = [(j, s) for s in range(1, subs)] + [(r, 0) for r in fresh]
        arrived = handed + [ring[r] for r in fresh]
        partial = run_experts(after, weights, sources, arrived, tables, kinds, slots)
        firsts.append(partial[0])
        if j == 0:
            held = near
            while 2 ** len(weights) < 2 * depth:
                moved = shift(held, "z", 2 ** (len(weights) - 1))
                weights.append(follow(moved, partial[0]))
                held = jnp.concatenate([held, weights[-1]], axis=0)
        if len(ring) == j + 2 < depth:
            ring.append(follow(shift(ring[-1], "z", 1), partial[0]))
        if j == 1:
            joint, *partial = partial
            fresh = fresh[1:]
        else:
            others[j], partial = partial[: subs - 1], partial[subs - 1 :]
        for r, rows in zip(fresh, partial):
            kept[r] = rows
    home, joined = kept[0], others[0]
    if depth > 1:
        sent = follow(shift(follow(joint, ring[last]), "z", -1), firsts[-1])
        sent = [sent[s * block : (s + 1) * block].astype(jnp.float32) for s in range(subs)]
        joined = [
            (mine.astype(jnp.float32) + rows).astype(jnp.bfloat16)
            for mine, rows in zip(others[0], sent)
        ]
        home = home + sent[-1]
    for r in range(2, depth):
        if r not in totals:
            behind = [firsts[-1]] + ([totals[r - 1]] * (r > 2) + [home, *joined] if r == last else [])
            totals[r] = total(r, *behind).astype(jnp.bfloat16)
    came = []
    for r in range(2, depth):
        rows = shift(totals[r], "z", -r)
        came.append(follow(rows, came[-1]) if came else rows)
    for s, rows in enumerate(joined, 1):
        if came:
            rows = follow(shift(follow(rows, totals[last]), "sub", -s), came[-1])
        else:
            rows = shift(rows, "sub", -s)
        home = home + rows.astype(jnp.float32)
    for rows in came:
        home = home + rows.astype(jnp.float32)
    return home.astype(jnp.bfloat16)


def solution(mesh):
    groups, experts, sub = (mesh.shape[a] for a in ("groups", "expert", "sub"))
    inner = Mesh(
        mesh.devices.reshape(groups, experts // CORES, CORES, sub),
        ("groups", "z", "core", "sub"),
    )
    tokens = P(("groups", "z", "core", "sub"), None)
    table = P(("z", "core"), None, "sub")
    return jax.shard_map(
        local,
        mesh=inner,
        in_specs=(tokens, tokens, tokens, table, table),
        out_specs=tokens,
        check_vma=False,
    )
```
